32 devices in a mesh: fsdp: 4 (over z), ctx: 4 (over x, core), tp: 2 (over y).
Axes of the slice: x: 2, y: 2, z: 4, core: 2. Of those that a mesh axis runs over, the one named last changes fastest.
Arguments:
- hidden_in: bfloat16 [8, 1024, 1024], P('fsdp', 'ctx'), may hold values from -6 to 6
- encoder_states: bfloat16 [8, 512, 1024], P('fsdp', 'ctx'), may hold values from -6 to 6
- dec_segments: int32 [8, 1024], P('fsdp'), may hold values from 0 to 7, as said below
- enc_segments: int32 [8, 512], P('fsdp'), may hold values from 0 to 7, as said below
- bucket_table: int32 [1024], replicated, may hold values from 0 to 31, as said below
- out_cotangent: bfloat16 [8, 1024, 1024], P('fsdp', 'ctx'), may hold values from -6 to 6
- self_gain: bfloat16 [1024], P('fsdp'), may hold values from 0.25 to 1.75
- self_query: bfloat16 [1024, 1024], P('fsdp', 'tp'), may hold values from -0.0234375 to 0.0234375
- self_key: bfloat16 [1024, 1024], P('fsdp', 'tp'), may hold values from -0.1875 to 0.1875
- self_value: bfloat16 [1024, 1024], P('fsdp', 'tp'), may hold values from -0.1875 to 0.1875
- self_output: bfloat16 [1024, 1024], P('tp', 'fsdp'), may hold values from -1 to 1
- position_bias: bfloat16 [32, 16], P('fsdp', 'tp'), may hold values from -4 to 4
- cross_gain: bfloat16 [1024], P('fsdp'), may hold values from 0.25 to 1.75
- cross_query: bfloat16 [1024, 1024], P('fsdp', 'tp'), may hold values from -0.0234375 to 0.0234375
- cross_key: bfloat16 [1024, 1024], P('fsdp', 'tp'), may hold values from -0.1875 to 0.1875
- cross_value: bfloat16 [1024, 1024], P('fsdp', 'tp'), may hold values from -0.1875 to 0.1875
- cross_output: bfloat16 [1024, 1024], P('tp', 'fsdp'), may hold values from -1 to 1
- ffn_gain: bfloat16 [1024], P('fsdp'), may hold values from 0.25 to 1.75
- ffn_gate: bfloat16 [1024, 2816], P('fsdp', 'tp'), may hold values from -0.1875 to 0.1875
- ffn_up: bfloat16 [1024, 2816], P('fsdp', 'tp'), may hold values from -0.1875 to 0.1875
- ffn_down: bfloat16 [2816, 1024], P('tp', 'fsdp'), may hold values from -0.15625 to 0.15625
Outputs:
- layer_output: bfloat16 [8, 1024, 1024], P('fsdp', 'ctx')
- grad_hidden: bfloat16 [8, 1024, 1024], P('fsdp', 'ctx')
- grad_encoder: bfloat16 [8, 512, 1024], P('fsdp', 'ctx')
- grad_self_gain: float32 [1024], P('fsdp')
- grad_self_query: float32 [1024, 1024], P('fsdp', 'tp')
- grad_self_key: float32 [1024, 1024], P('fsdp', 'tp')
- grad_self_value: float32 [1024, 1024], P('fsdp', 'tp')
- grad_self_output: float32 [1024, 1024], P('tp', 'fsdp')
- grad_position_bias: float32 [32, 16], P('fsdp', 'tp')
- grad_cross_gain: float32 [1024], P('fsdp')
- grad_cross_query: float32 [1024, 1024], P('fsdp', 'tp')
- grad_cross_key: float32 [1024, 1024], P('fsdp', 'tp')
- grad_cross_value: float32 [1024, 1024], P('fsdp', 'tp')
- grad_cross_output: float32 [1024, 1024], P('tp', 'fsdp')
- grad_ffn_gain: float32 [1024], P('fsdp')
- grad_ffn_gate: float32 [1024, 2816], P('fsdp', 'tp')
- grad_ffn_up: float32 [1024, 2816], P('fsdp', 'tp')
- grad_ffn_down: float32 [2816, 1024], P('tp', 'fsdp')
The draws below stay inside these ranges and needn't reach their ends.
Inputs may be any that keep to these rules, and one draw needn't show every extreme that they name: `dec_segments`: each row gives the document of every decoder position of a sequence: 0 at the first position, never falling, rising by at most one from a position to the next. In each aligned block of 2 rows, one row's last document begins before position 128. `enc_segments`: each row gives the document of every encoder position of the same sequence: 0 at the first position, never falling, rising by at most one at a time, and with the same last number as the decoder row, so that every decoder document has encoder positions. `bucket_table`: entry d is the bucket of a key d positions before its query; 0 at d = 0, never falling.
All inputs are finite; a program needn't handle non-finite values.
Results may differ from the reference program's by a relative error of at most 0.033.
Values may be sent and summed in bfloat16 or wider, within the bound.
No kernel may reach another device: no remote copies, remote signals or barrier semaphores. Data moves between devices by JAX's collectives and lax.ppermute only.
A program may use at most 192 MiB of HBM per device.

```python
import jax
import jax.numpy as jnp
from jax import lax

D = 1024
HEADS = 16
HEAD_DIM = 64
FF = 2816
NB = 32
LEN = 1024
ENC_LEN = 512
SEQ_DEV = 2
SEQS = 8
N_TP = 2


def document_plan(source_key):
    key_count_total = jax.random.fold_in(source_key, 101)
    chosen_key = jax.random.fold_in(source_key, 102)
    rows_all = jnp.arange(SEQS, dtype=jnp.int32)
    counts = jax.random.randint(key_count_total, (SEQS,), 1, 9)
    counts = jnp.where(rows_all == 0, 8, counts).astype(jnp.int32)
    offsets = jax.random.randint(chosen_key, (SEQS // SEQ_DEV,), 0, SEQ_DEV)
    chosen = rows_all % SEQ_DEV == jnp.repeat(offsets, SEQ_DEV)
    return (counts, chosen)


def document_cuts(source_key, extent, limits, counts):
    row_total = limits.shape[0]
    row_keys = jax.random.split(source_key, row_total)
    orders = jax.vmap(lambda row_key: jax.random.permutation(row_key, extent - 1))(row_keys).astype(jnp.int32)
    places = jnp.arange(1, extent, dtype=jnp.int32)
    scores = orders + jnp.where(places[None, :] < limits[:, None], 0, extent).astype(jnp.int32)
    rank_order = jnp.argsort(jnp.argsort(scores, axis=1, stable=True), axis=1, stable=True)
    cut_marks = (rank_order < counts[:, None] - 1).astype(jnp.int32)
    starts = jnp.zeros((row_total, 1), jnp.int32)
    return jnp.cumsum(jnp.concatenate([starts, cut_marks], axis=1), axis=1).astype(jnp.int32)


def draw_dec_segments(key, part):
    counts, chosen = document_plan(key)
    key = jax.random.fold_in(key, 7)
    limits = jnp.where(chosen, LEN // 8, LEN).astype(jnp.int32)
    return document_cuts(key, LEN, limits, counts)


def draw_enc_segments(key, part):
    counts, chosen = document_plan(key)
    key = jax.random.fold_in(key, 11)
    limits = jnp.full((SEQS,), ENC_LEN, jnp.int32)
    return document_cuts(key, ENC_LEN, limits, counts)


def draw_bucket_table(key, part):
    key = jax.random.fold_in(key, 13)
    steps_up = jax.random.randint(key, (LEN,), 1, 4)
    climbed = jnp.cumsum(steps_up) - steps_up[0]
    return (climbed * NB // (climbed[-1] + 1)).astype(jnp.int32)


def block_levels(stream_key, dims, cuts, low, high):
    def one(position, parts):
        steps = jax.random.uniform(jax.random.fold_in(jax.random.fold_in(stream_key, 6), position), (parts,), jnp.float32, low / len(cuts), high / len(cuts))
        return jnp.repeat(jnp.exp(steps), dims[position] // parts).reshape((-1,) + (1,) * (len(dims) - position - 1))

    factor_of = one(*cuts[0])
    for cut in cuts[1:]:
        factor_of = factor_of * one(*cut)
    return factor_of


def bell_draw(key, dims, width, limit, cuts=(), kind=jnp.bfloat16):
    level = block_levels(key, dims, cuts, -0.22, 0.18) if cuts else 1.0
    entries = jax.random.normal(key, dims, jnp.float32) * width * level
    return jnp.minimum(jnp.maximum(entries, -limit), limit).astype(kind)


def setup_inputs(seed: int = 0) -> dict:
    streams_of = jax.random.split(jax.random.key(seed), 22)
    hidden_in = bell_draw(streams_of[0], (SEQS, LEN, D), 1.0, 6.0, ((0, 4), (1, 4)))
    encoder_states = bell_draw(streams_of[1], (SEQS, ENC_LEN, D), 1.0, 6.0, ((0, 4), (1, 4)))
    dec_segments = draw_dec_segments(jax.random.fold_in(streams_of[21], 71), 0)
    enc_segments = draw_enc_segments(jax.random.fold_in(streams_of[21], 71), 0)
    bucket_table = draw_bucket_table(jax.random.fold_in(streams_of[21], 71), 0)
    out_cotangent = bell_draw(streams_of[5], (SEQS, LEN, D), 1.0, 6.0, ((0, 4), (1, 4)))
    self_gain = jnp.clip(1.0 + 0.15 * jax.random.normal(streams_of[6], (D,), jnp.float32), 0.25, 1.75).astype(jnp.bfloat16)
    self_query = bell_draw(streams_of[7], (D, HEADS * HEAD_DIM), (D * HEAD_DIM) ** -0.5, 0.0234375, ((0, 4), (1, 2)))
    self_key = bell_draw(streams_of[8], (D, HEADS * HEAD_DIM), D ** -0.5, 0.1875, ((0, 4), (1, 2)))
    self_value = bell_draw(streams_of[9], (D, HEADS * HEAD_DIM), D ** -0.5, 0.1875, ((0, 4), (1, 2)))
    self_output = bell_draw(streams_of[10], (HEADS * HEAD_DIM, D), (HEADS * HEAD_DIM // 32) ** -0.5, 1.0, ((0, 2), (1, 4)))
    position_bias = bell_draw(streams_of[11], (NB, HEADS), 1.0, 4.0, ((0, 4), (1, 2)))
    cross_gain = jnp.clip(1.0 + 0.15 * jax.random.normal(streams_of[12], (D,), jnp.float32), 0.25, 1.75).astype(jnp.bfloat16)
    cross_query = bell_draw(streams_of[13], (D, HEADS * HEAD_DIM), (D * HEAD_DIM) ** -0.5, 0.0234375, ((0, 4), (1, 2)))
    cross_key = bell_draw(streams_of[14], (D, HEADS * HEAD_DIM), D ** -0.5, 0.1875, ((0, 4), (1, 2)))
    cross_value = bell_draw(streams_of[15], (D, HEADS * HEAD_DIM), D ** -0.5, 0.1875, ((0, 4), (1, 2)))
    cross_output = bell_draw(streams_of[16], (HEADS * HEAD_DIM, D), (HEADS * HEAD_DIM // 32) ** -0.5, 1.0, ((0, 2), (1, 4)))
    ffn_gain = jnp.clip(1.0 + 0.15 * jax.random.normal(streams_of[17], (D,), jnp.float32), 0.25, 1.75).astype(jnp.bfloat16)
    ffn_gate = bell_draw(streams_of[18], (D, FF), D ** -0.5, 0.1875, ((0, 4), (1, 2)))
    ffn_up = bell_draw(streams_of[19], (D, FF), D ** -0.5, 0.1875, ((0, 4), (1, 2)))
    ffn_down = bell_draw(streams_of[20], (FF, D), (FF // 2) ** -0.5, 0.15625, ((0, 2), (1, 4)))
    return {"hidden_in": hidden_in, "encoder_states": encoder_states, "dec_segments": dec_segments, "enc_segments": enc_segments, "bucket_table": bucket_table, "out_cotangent": out_cotangent, "self_gain": self_gain, "self_query": self_query, "self_key": self_key, "self_value": self_value, "self_output": self_output, "position_bias": position_bias, "cross_gain": cross_gain, "cross_query": cross_query, "cross_key": cross_key, "cross_value": cross_value, "cross_output": cross_output, "ffn_gain": ffn_gain, "ffn_gate": ffn_gate, "ffn_up": ffn_up, "ffn_down": ffn_down}


EPSILON = 1e-06
NEGATIVE = -1e+30

@jax.custom_vjp
def low(v):
    return lax.optimization_barrier(v.astype(jnp.bfloat16)).astype(jnp.float32)

@jax.custom_vjp
def low_back(v):
    return v

def low_keep(v):
    return (low(v), None)

def low_pass(kept, grad):
    return (grad,)

def back_keep(v):
    return (v, None)

def back_low(kept, grad):
    return (low(grad),)
low.defvjp(low_keep, low_pass)
low_back.defvjp(back_keep, back_low)

def matmul(first_factor, second_factor):
    return jnp.dot(first_factor, second_factor, precision=lax.Precision.HIGHEST)

def norm_apply(values, gain_row):
    inverse_rms = lax.rsqrt(lax.optimization_barrier(jnp.mean(values * values, axis=-1, keepdims=True)) + EPSILON)
    return values * inverse_rms * gain_row

def attend(query_rows, key_rows, value_rows, score_bias, visible):
    query_heads = query_rows.reshape(query_rows.shape[0], HEADS, HEAD_DIM)
    key_heads = key_rows.reshape(key_rows.shape[0], HEADS, HEAD_DIM)
    value_heads = value_rows.reshape(value_rows.shape[0], HEADS, HEAD_DIM)
    scores = jnp.einsum('qhe,khe->hqk', query_heads, key_heads, precision=lax.Precision.HIGHEST) + score_bias
    scores = jnp.where(visible[None], low_back(scores), NEGATIVE)
    weights = low(jax.nn.softmax(scores, axis=-1))
    attended = jnp.einsum('hqk,khe->qhe', weights, value_heads, precision=lax.Precision.HIGHEST)
    return low_back(low(attended.reshape(query_rows.shape[0], HEADS * HEAD_DIM)))

def branch(input_rows, weight_matrix):
    groups = input_rows.reshape(input_rows.shape[0], N_TP, -1)
    blocks = weight_matrix.reshape(N_TP, -1, weight_matrix.shape[1])
    running = jnp.zeros((input_rows.shape[0], weight_matrix.shape[1]), jnp.float32)
    for member in range(N_TP):
        running = running + low(matmul(groups[:, member], blocks[member]))
    return low_back(running)

def layer(hidden, encoder, decoder_documents, encoder_docs, buckets, weight_set):
    gain_self, query_self, key_self, self_value_weight, output_self, bias_table, gain_cross, query_cross, key_cross, value_cross, output_cross, gain_ffn, gate_ffn, up_ffn, down_ffn = weight_set
    positions = jnp.arange(LEN, dtype=jnp.int32)
    distance = jnp.clip(positions[:, None] - positions[None, :], 0, LEN - 1).astype(jnp.int32)
    score_bias = jnp.transpose(bias_table[buckets[distance]], (2, 0, 1))
    self_visible = (positions[:, None] >= positions[None, :]) & (decoder_documents[:, None] == decoder_documents[None, :])
    cross_visible = decoder_documents[:, None] == encoder_docs[None, :]
    normed = low(norm_apply(hidden, gain_self))
    query_rows = low_back(low(matmul(normed, query_self)))
    key_rows = low_back(low(matmul(normed, key_self)))
    value_rows = low_back(low(matmul(normed, self_value_weight)))
    after_one = hidden + branch(attend(query_rows, key_rows, value_rows, score_bias, self_visible), output_self)
    normed = low(norm_apply(after_one, gain_cross))
    query_rows = low_back(low(matmul(normed, query_cross)))
    key_rows = low_back(low(matmul(encoder, key_cross)))
    value_rows = low_back(low(matmul(encoder, value_cross)))
    after_two = after_one + branch(attend(query_rows, key_rows, value_rows, 0.0, cross_visible), output_cross)
    normed = low(norm_apply(after_two, gain_ffn))
    gate_rows = low_back(matmul(normed, gate_ffn))
    upward = low_back(matmul(normed, up_ffn))
    hidden_units = low(jax.nn.gelu(gate_rows, approximate=True) * upward)
    return after_two + branch(hidden_units, down_ffn)

def reference(hidden_in, encoder_states, dec_segments, enc_segments, bucket_table, out_cotangent, self_gain, self_query, self_key, self_value, self_output, position_bias, cross_gain, cross_query, cross_key, cross_value, cross_output, ffn_gain, ffn_gate, ffn_up, ffn_down):
    weight_set = tuple((tensor.astype(jnp.float32) for tensor in (self_gain, self_query, self_key, self_value, self_output, position_bias, cross_gain, cross_query, cross_key, cross_value, cross_output, ffn_gain, ffn_gate, ffn_up, ffn_down)))

    def one_sequence(running, slices):
        hidden, encoder, decoder_documents, encoder_docs, cotangent = slices

        def forward(hidden_value, encoder_value, weight_value):
            return layer(hidden_value, encoder_value, decoder_documents, encoder_docs, bucket_table, weight_value)
        output, pullback = jax.vjp(forward, hidden.astype(jnp.float32), encoder.astype(jnp.float32), weight_set)
        grad_input, grad_states, grad_weights = pullback(cotangent.astype(jnp.float32))
        running = jax.tree.map(jnp.add, running, grad_weights)
        return (running, (output.astype(jnp.bfloat16), grad_input.astype(jnp.bfloat16), grad_states.astype(jnp.bfloat16)))
    starting = jax.tree.map(jnp.zeros_like, weight_set)
    gradient_list, (outputs, grad_inputs, grad_states) = lax.scan(one_sequence, starting, (hidden_in, encoder_states, dec_segments, enc_segments, out_cotangent))
    return (outputs, grad_inputs, grad_states, gradient_list[0], gradient_list[1], gradient_list[2], gradient_list[3], gradient_list[4], gradient_list[5], gradient_list[6], gradient_list[7], gradient_list[8], gradient_list[9], gradient_list[10], gradient_list[11], gradient_list[12], gradient_list[13], gradient_list[14])
```

```python
import functools
import jax
import jax.numpy as jnp
from jax import lax
from jax.experimental import pallas as pl
from jax.experimental.pallas import tpu as pltpu
from jax.sharding import PartitionSpec as P

EPSILON = 1e-06
NEGATIVE = -1e30
LANES = 128
CHUNK = 256
NT = (((1,), (1,)), ((), ()))
NN = (((1,), (0,)), ((), ()))


def dot(lhs, rhs, dims=NN):
    return lax.dot_general(lhs, rhs, dims, preferred_element_type=jnp.float32)


def fill_mask(mask_ref, seg_row, seg_col_ref, offset_ref, causal):
    rows = seg_row.shape[1]
    keys = mask_ref.shape[0]
    for start in range(0, keys, CHUNK):
        size = min(CHUNK, keys - start)
        seen = seg_col_ref[0, pl.ds(start, size), :] == seg_row
        if causal:
            key_place = lax.broadcasted_iota(jnp.int32, (size, rows), 0) + start
            query_place = lax.broadcasted_iota(jnp.int32, (size, rows), 1) + offset_ref[0, 0]
            seen = seen & (key_place <= query_place)
        mask_ref[pl.ds(start, size), :] = jnp.where(seen, 0.0, NEGATIVE)


def fill_bias(bias_ref, head, line):
    width = line.shape[1]
    base = jnp.broadcast_to(line, (8, width))
    row = lax.broadcasted_iota(jnp.int32, (8, width), 0)
    for bit in (1, 2, 4):
        base = jnp.where((row & bit) != 0, pltpu.roll(base, bit, 1), base)
    for block in range(LANES // 8):
        bias_ref[head, pl.ds(8 * block, 8), :] = pltpu.roll(base, 8 * block, 1) if block else base


def fold_diagonals(total):
    width = total.shape[1]
    half = total.shape[0] // 2
    while half >= 8:
        total = total[:half] + pltpu.roll(total[half:], width - half, 1)
        half //= 2
    row = lax.broadcasted_iota(jnp.int32, (8, width), 0)
    for bit in (4, 2, 1):
        total = jnp.where((row & bit) != 0, pltpu.roll(total, width - bit, 1), total)
    return jnp.sum(total, axis=0, keepdims=True)


def head_mask(rows, head):
    lane = lax.broadcasted_iota(jnp.int32, (rows, LANES), 1)
    return (lane // (LANES // 2)) == head


def add_bias(scores, bias_ref, head, start, keys, rows):
    parts = []
    for sub in range(0, scores.shape[0], LANES):
        at = keys - (start + sub)
        parts.append(scores[sub : sub + LANES] + bias_ref[head, :, at : at + rows])
    return jnp.concatenate(parts, axis=0)


def forward_kernel(causal, *refs):
    if causal:
        (offset_ref, line_ref, seg_row_ref, seg_col_ref, q_ref, k_ref, v_ref, out_ref, log_ref,
         mask_ref, score_ref, bias_ref) = refs
    else:
        (seg_row_ref, seg_col_ref, q_ref, k_ref, v_ref, out_ref, log_ref,
         mask_ref, score_ref) = refs
        offset_ref = None
    pair = pl.program_id(0)
    seq = pl.program_id(1)
    rows = q_ref.shape[1]
    keys = k_ref.shape[1]

    @pl.when(pair == 0)
    def _():
        fill_mask(mask_ref.at[seq], seg_row_ref[0], seg_col_ref, offset_ref, causal)

    if causal:

        @pl.when(seq == 0)
        def _():
            for head in range(2):
                fill_bias(bias_ref, head, line_ref[0, pl.ds(head, 1), :])

    q = q_ref[0]
    v_turned = v_ref[0].T
    half = LANES // 2
    outs = []
    logs = []
    for head in range(2):
        q_head = jnp.where(head_mask(rows, head), q, jnp.zeros_like(q))
        highest = None
        for start in range(0, keys, CHUNK):
            scores = dot(k_ref[0, pl.ds(start, CHUNK), :], q_head, NT)
            scores = scores + mask_ref[seq, pl.ds(start, CHUNK), :]
            if causal:
                scores = add_bias(scores, bias_ref, head, start, keys, rows)
            score_ref[pl.ds(start, CHUNK), :] = scores
            top = jnp.max(scores, axis=0, keepdims=True)
            highest = top if highest is None else jnp.maximum(highest, top)
        total = None
        attended = None
        for start in range(0, keys, CHUNK):
            grown = jnp.exp(score_ref[pl.ds(start, CHUNK), :] - highest)
            part = jnp.sum(grown, axis=0, keepdims=True)
            piece = dot(v_turned[half * head : half * head + half, start : start + CHUNK],
                        grown.astype(jnp.bfloat16))
            total = part if total is None else total + part
            attended = piece if attended is None else attended + piece
        outs.append(attended / total)
        logs.append(highest + jnp.log(total))
    out_ref[0] = jnp.concatenate(outs, axis=0).T.astype(jnp.bfloat16)
    log_ref[0, 0] = jnp.concatenate(logs + [jnp.zeros((6, rows), jnp.float32)], axis=0)


def backward_kernel(causal, *refs):
    if causal:
        (offset_ref, line_ref, seg_row_ref, seg_col_ref, q_ref, k_ref, v_ref, out_ref, log_ref,
         grad_ref, dq_ref, dk_ref, dv_ref, line_grad_ref, mask_ref, bias_ref, total_ref) = refs
    else:
        (seg_row_ref, seg_col_ref, q_ref, k_ref, v_ref, out_ref, log_ref,
         grad_ref, dq_ref, dk_ref, dv_ref, mask_ref) = refs
        offset_ref = None
    pair = pl.program_id(0)
    seq = pl.program_id(1)
    rows = q_ref.shape[1]
    keys = k_ref.shape[1]
    half = LANES // 2

    @pl.when(pair == 0)
    def _():
        fill_mask(mask_ref.at[seq], seg_row_ref[0], seg_col_ref, offset_ref, causal)

    if causal:

        @pl.when(seq == 0)
        def _():
            for head in range(2):
                fill_bias(bias_ref, head, line_ref[0, pl.ds(head, 1), :])
            total_ref[...] = jnp.zeros_like(total_ref)

    q = q_ref[0]
    grad = grad_ref[0]
    product = grad.astype(jnp.float32) * out_ref[0].astype(jnp.float32)
    chooser = (
        lax.broadcasted_iota(jnp.int32, (8, LANES), 1) // half
        == lax.broadcasted_iota(jnp.int32, (8, LANES), 0)
    ).astype(jnp.float32)
    inner = lax.dot_general(chooser, product, NT, precision=lax.Precision.HIGHEST,
                            preferred_element_type=jnp.float32)
    q_heads = [jnp.where(head_mask(rows, h), q, jnp.zeros_like(q)) for h in range(2)]
    grad_heads = [jnp.where(head_mask(rows, h), grad, jnp.zeros_like(grad)) for h in range(2)]
    dq = [None, None]
    for start in range(0, keys, CHUNK):
        k = k_ref[0, pl.ds(start, CHUNK), :]
        v = v_ref[0, pl.ds(start, CHUNK), :]
        k_turned = k.T
        dk = None
        dv = None
        for head in range(2):
            scores = dot(k, q_heads[head], NT)
            scores = scores + mask_ref[seq, pl.ds(start, CHUNK), :]
            if causal:
                scores = add_bias(scores, bias_ref, head, start, keys, rows)
            weights = jnp.exp(scores - log_ref[0, 0, pl.ds(head, 1), :])
            dv_part = dot(weights.astype(jnp.bfloat16), grad_heads[head])
            dw = dot(v, grad_heads[head], NT)
            ds = weights * (dw - inner[head : head + 1])
            ds_low = ds.astype(jnp.bfloat16)
            dk_part = dot(ds_low, q_heads[head])
            dq_part = dot(k_turned[half * head : half * head + half], ds_low)
            dv = dv_part if dv is None else dv + dv_part
            dk = dk_part if dk is None else dk + dk_part
            dq[head] = dq_part if dq[head] is None else dq[head] + dq_part
            if causal:
                for sub in range(0, CHUNK, LANES):
                    at = keys - (start + sub)
                    total_ref[head, :, at : at + rows] += ds[sub : sub + LANES]
        dk_ref[0, pl.ds(start, CHUNK), :] = dk.astype(jnp.bfloat16)
        dv_ref[0, pl.ds(start, CHUNK), :] = dv.astype(jnp.bfloat16)
    dq_ref[0] = jnp.concatenate(dq, axis=0).T.astype(jnp.bfloat16)
    if causal:

        @pl.when(seq == pl.num_programs(1) - 1)
        def _():
            lines = [fold_diagonals(total_ref[head]) for head in range(2)]
            lines.append(jnp.zeros((6, lines[0].shape[1]), jnp.float32))
            line_grad_ref[0] = jnp.concatenate(lines, axis=0)


def specs_for(rows, keys, pairs, causal):
    def wide(count, shift=0):
        return pl.BlockSpec((1, count, LANES), lambda p, s: (s, 0, p + shift))

    lead = []
    if causal:
        lead = [
            pl.BlockSpec((1, 1), lambda p, s: (0, 0), memory_space=pltpu.SMEM),
            pl.BlockSpec((1, 8, rows + keys), lambda p, s: (p, 0, 0)),
        ]
    lead += [
        pl.BlockSpec((1, 1, rows), lambda p, s: (s, 0, 0)),
        pl.BlockSpec((1, keys, 1), lambda p, s: (s, 0, 0)),
        wide(rows),
        wide(keys),
        wide(keys, pairs),
    ]
    return lead, wide, pl.BlockSpec((1, 1, 8, rows), lambda p, s: (s, p, 0, 0))


def attend_forward(q, kv, seg_row, seg_col, offset=None, lines=None):
    seqs, rows, width = q.shape
    keys = kv.shape[1]
    pairs = width // LANES
    causal = lines is not None
    lead, wide, logs = specs_for(rows, keys, pairs, causal)
    scratch = [pltpu.VMEM((seqs, keys, rows), jnp.float32), pltpu.VMEM((keys, rows), jnp.float32)]
    args = [seg_row, seg_col, q, kv, kv]
    if causal:
        args = [offset, lines] + args
        scratch.append(pltpu.VMEM((2, LANES, rows + keys), jnp.float32))
    return pl.pallas_call(
        functools.partial(forward_kernel, causal),
        grid=(pairs, seqs),
        in_specs=lead,
        out_specs=[wide(rows), logs],
        out_shape=[
            jax.ShapeDtypeStruct((seqs, rows, width), jnp.bfloat16),
            jax.ShapeDtypeStruct((seqs, pairs, 8, rows), jnp.float32),
        ],
        scratch_shapes=scratch,
        compiler_params=pltpu.CompilerParams(vmem_limit_bytes=40 * 1024 * 1024),
        cost_estimate=pl.CostEstimate(
            flops=seqs * pairs * 4 * 2 * rows * keys * 128,
            bytes_accessed=4 * seqs * (rows + keys) * width,
            transcendentals=seqs * pairs * 2 * rows * keys,
        ),
        name="attend_forward",
    )(*args)


def attend_backward(q, kv, seg_row, seg_col, out, logs_value, grad, offset=None, lines=None):
    seqs, rows, width = q.shape
    keys = kv.shape[1]
    pairs = width // LANES
    causal = lines is not None
    lead, wide, logs = specs_for(rows, keys, pairs, causal)
    scratch = [pltpu.VMEM((seqs, keys, rows), jnp.float32)]
    args = [seg_row, seg_col, q, kv, kv, out, logs_value, grad]
    out_shape = [
        jax.ShapeDtypeStruct((seqs, rows, width), jnp.bfloat16),
        jax.ShapeDtypeStruct((seqs, keys, width), jnp.bfloat16),
        jax.ShapeDtypeStruct((seqs, keys, width), jnp.bfloat16),
    ]
    out_specs = [wide(rows), wide(keys), wide(keys)]
    if causal:
        args = [offset, lines] + args
        scratch.append(pltpu.VMEM((2, LANES, rows + keys), jnp.float32))
        scratch.append(pltpu.VMEM((2, LANES, rows + keys), jnp.float32))
        out_shape.append(jax.ShapeDtypeStruct((pairs, 8, rows + keys), jnp.float32))
        out_specs.append(pl.BlockSpec((1, 8, rows + keys), lambda p, s: (p, 0, 0)))
    return pl.pallas_call(
        functools.partial(backward_kernel, causal),
        grid=(pairs, seqs),
        in_specs=lead + [wide(rows), logs, wide(rows)],
        out_specs=out_specs,
        out_shape=out_shape,
        scratch_shapes=scratch,
        compiler_params=pltpu.CompilerParams(vmem_limit_bytes=40 * 1024 * 1024),
        cost_estimate=pl.CostEstimate(
            flops=seqs * pairs * 10 * 2 * rows * keys * 128,
            bytes_accessed=8 * seqs * (rows + keys) * width,
            transcendentals=seqs * pairs * 2 * rows * keys,
        ),
        name="attend_backward",
    )(*args)


def mm(lhs, rhs):
    return lax.dot_general(lhs, rhs, (((lhs.ndim - 1,), (0,)), ((), ())),
                           preferred_element_type=jnp.float32)


def mm_back(lhs, rhs):
    return lax.dot_general(lhs, rhs, (((lhs.ndim - 1,), (1,)), ((), ())),
                           preferred_element_type=jnp.float32)


def weight_grad(rows, grads):
    return lax.dot_general(rows, grads, (((0, 1), (0, 1)), ((), ())),
                           preferred_element_type=jnp.float32).astype(jnp.bfloat16)


def rms_forward(values, gain_row):
    inverse_rms = lax.rsqrt(jnp.mean(values * values, axis=-1, keepdims=True) + EPSILON)
    unit_rows = values * inverse_rms
    return unit_rows, inverse_rms, (unit_rows * gain_row).astype(jnp.bfloat16)


def rms_backward(grad_normed, unit_rows, inverse_rms, gain_row):
    grad_unit = grad_normed * gain_row
    grad_gain = jnp.sum(grad_normed * unit_rows, axis=(0, 1))
    inner_sum = jnp.mean(grad_unit * unit_rows, axis=-1, keepdims=True)
    return inverse_rms * (grad_unit - unit_rows * inner_sum), grad_gain


def ctx_shape():
    count = lax.axis_size("ctx")
    low = 2 if count % 2 == 0 else 1
    return count // low, low


def ctx_place():
    high, low = ctx_shape()
    index = lax.axis_index("ctx")
    return index // low, index % low


def swap_low(value):
    high, low = ctx_shape()
    return lax.ppermute(value, "ctx", [(i, i ^ 1) for i in range(high * low)])


def shift_high(value, step, wrap):
    high, low = ctx_shape()
    pairs = []
    for i in range(high * low):
        target = i // low + step
        if wrap or 0 <= target < high:
            pairs.append((i, (target % high) * low + i % low))
    return lax.ppermute(value, "ctx", pairs)


def ctx_gather(value, axis, causal):
    high, low = ctx_shape()
    at_high, at_low = ctx_place()
    got = [value] + [shift_high(value, step, not causal) for step in range(1, high)]
    slots = []
    for slot in range(high):
        block = jnp.zeros_like(value) if causal else value
        for place in range(high):
            if place >= slot or not causal:
                block = jnp.where(at_high == place, got[(place - slot) % high], block)
        slots.append(block)
    held = jnp.stack(slots, axis)
    if low == 2:
        other = swap_low(held)
        first = jnp.where(at_low == 0, held, other)
        second = jnp.where(at_low == 0, other, held)
        held = jnp.stack([first, second], axis + 1)
    shape = value.shape[:axis] + (high * low * value.shape[axis],) + value.shape[axis + 1 :]
    return held.reshape(shape)


def ctx_fold(value, axis, causal):
    high, low = ctx_shape()
    at_high, at_low = ctx_place()
    size = value.shape[axis] // (high * low)
    view = value.reshape(value.shape[:axis] + (high, low, size) + value.shape[axis + 1 :])
    if low == 2:
        mine = lax.dynamic_index_in_dim(view, at_low, axis + 1, False)
        other = swap_low(lax.dynamic_index_in_dim(view, 1 - at_low, axis + 1, False))
        held = (mine.astype(jnp.float32) + other.astype(jnp.float32)).astype(jnp.bfloat16)
    else:
        held = lax.squeeze(view, (axis + 1,))
    total = lax.dynamic_index_in_dim(held, at_high, axis, False).astype(jnp.float32)
    for step in range(1, high):
        target = at_high - step
        piece = lax.dynamic_index_in_dim(held, target % high, axis, False)
        total = total + shift_high(piece, -step, not causal).astype(jnp.float32)
    return total


def gather_rows(shards):
    count = lax.axis_size("ctx")
    rows = shards[0].shape[0] // count
    start = lax.axis_index("ctx") * rows
    parts = [lax.dynamic_slice_in_dim(s, start, rows, 0) for s in shards]
    part = jnp.concatenate(parts, axis=1) if len(parts) > 1 else parts[0]
    return lax.all_gather(part, ("fsdp", "ctx"), axis=0, tiled=True)


def scatter_rows(grads):
    part = lax.psum_scatter(grads, ("fsdp", "ctx"), scatter_dimension=0, tiled=True)
    return ctx_gather(part, 0, False).astype(jnp.float32)


def pair_total(partial):
    own = partial.astype(jnp.bfloat16)
    count = lax.axis_size("tp")
    total = own.astype(jnp.float32)
    for step in range(1, count):
        moved = lax.ppermute(own, "tp", [(i, (i + step) % count) for i in range(count)])
        total = total + moved.astype(jnp.float32)
    return total


def body(
    hidden_in,
    encoder_states,
    dec_segments,
    enc_segments,
    bucket_table,
    out_cotangent,
    self_gain,
    self_query,
    self_key,
    self_value,
    self_output,
    position_bias,
    cross_gain,
    cross_query,
    cross_key,
    cross_value,
    cross_output,
    ffn_gain,
    ffn_gate,
    ffn_up,
    ffn_down,
):
    shards = lax.axis_size("fsdp")
    seq_count, row_count, width = hidden_in.shape
    length = dec_segments.shape[1]
    heads_width = self_query.shape[1]
    units = ffn_gate.shape[1]
    bucket_rows, head_count = position_bias.shape
    bucket_count = bucket_rows * shards
    gain_rows = self_gain.shape[0]
    offset = lax.axis_index("ctx") * row_count

    small = jnp.concatenate([self_gain, cross_gain, ffn_gain, position_bias.reshape(-1)])
    small = lax.all_gather(small, "fsdp", axis=0, tiled=False)
    gain_self, gain_cross, gain_ffn = [
        small[:, gain_rows * i : gain_rows * (i + 1)].reshape(width).astype(jnp.float32)
        for i in range(3)
    ]
    bias_table = small[:, 3 * gain_rows :].reshape(bucket_count, head_count).astype(jnp.float32)
    hidden_all = ctx_gather(hidden_in, 1, True)
    encoder_all = ctx_gather(encoder_states, 1, False)
    self_weights = gather_rows([self_query, self_key, self_value])
    middle_weights = gather_rows(
        [cross_query, cross_key, cross_value, self_output.T, cross_output.T]
    )
    ffn_weights = gather_rows([ffn_gate, ffn_up, ffn_down.T])
    query_self = self_weights[:, :heads_width]
    pair_self = self_weights[:, heads_width:]
    query_cross = middle_weights[:, :heads_width]
    pair_cross = middle_weights[:, heads_width : 3 * heads_width]
    output_self = middle_weights[:, 3 * heads_width : 4 * heads_width]
    output_cross = middle_weights[:, 4 * heads_width :]
    gate_up = ffn_weights[:, : 2 * units]
    down = ffn_weights[:, 2 * units :]

    query_docs = lax.dynamic_slice_in_dim(dec_segments, offset, row_count, 1)[:, None, :]
    dec_docs = dec_segments[:, :, None]
    enc_docs = enc_segments[:, :, None]
    bucket_onehot = (
        bucket_table[:, None] == jnp.arange(bucket_count, dtype=jnp.int32)[None, :]
    ).astype(jnp.float32)
    distance_bias = jnp.dot(bucket_onehot, bias_table, precision=lax.Precision.HIGHEST).T
    padded = jnp.concatenate([jnp.zeros_like(distance_bias), distance_bias], axis=1)
    lines = lax.dynamic_slice_in_dim(padded, offset, row_count + length, 1)
    lines = lines.reshape(head_count // 2, 2, row_count + length)
    lines = jnp.concatenate([lines, jnp.zeros_like(lines), jnp.zeros_like(lines),
                             jnp.zeros_like(lines)], axis=1)
    place = jnp.full((1, 1), offset, jnp.int32)

    source = hidden_in.astype(jnp.float32)
    unit_one, inverse_one, normed_one = rms_forward(source, gain_self)
    unused_unit, unused_inverse, normed_all = rms_forward(
        hidden_all.astype(jnp.float32), gain_self
    )
    queries_one = mm(normed_one, query_self).astype(jnp.bfloat16)
    pair_one = mm(normed_all, pair_self).astype(jnp.bfloat16)
    attended_one, logs_one = attend_forward(
        queries_one, pair_one, query_docs, dec_docs, place, lines
    )
    after_one = source + pair_total(mm_back(attended_one, output_self))

    pair_two = mm(encoder_all, pair_cross).astype(jnp.bfloat16)
    unit_two, inverse_two, normed_two = rms_forward(after_one, gain_cross)
    queries_two = mm(normed_two, query_cross).astype(jnp.bfloat16)
    attended_two, logs_two = attend_forward(queries_two, pair_two, query_docs, enc_docs)
    after_two = after_one + pair_total(mm_back(attended_two, output_cross))

    grad_units = mm(out_cotangent, down)
    unit_three, inverse_three, normed_three = rms_forward(after_two, gain_ffn)
    both_rows = mm(normed_three, gate_up)
    gate_rows = both_rows[..., :units]
    up_rows = both_rows[..., units:]
    activated, gelu_pull = jax.vjp(lambda v: jax.nn.gelu(v, approximate=True), gate_rows)
    hidden_units = (activated * up_rows).astype(jnp.bfloat16)
    grad_gate_rows = gelu_pull(grad_units * up_rows)[0].astype(jnp.bfloat16)
    grad_up_rows = (grad_units * activated).astype(jnp.bfloat16)
    grad_both = jnp.concatenate([grad_gate_rows, grad_up_rows], axis=-1)
    grad_normed = pair_total(mm_back(grad_both, gate_up))
    layer_output = after_two + pair_total(mm_back(hidden_units, down))
    grads_ffn = scatter_rows(
        jnp.concatenate(
            [weight_grad(normed_three, grad_both), weight_grad(out_cotangent, hidden_units)],
            axis=1,
        )
    )
    grad_from, grad_gain_ffn = rms_backward(grad_normed, unit_three, inverse_three, gain_ffn)
    grad_res = out_cotangent.astype(jnp.float32) + grad_from

    grad_low = grad_res.astype(jnp.bfloat16)
    grad_attended = mm(grad_low, output_cross).astype(jnp.bfloat16)
    grad_out_cross = weight_grad(grad_low, attended_two)
    grad_q_two, grad_k_two, grad_v_two = attend_backward(
        queries_two, pair_two, query_docs, enc_docs, attended_two, logs_two, grad_attended
    )
    grad_normed = pair_total(mm_back(grad_q_two, query_cross))
    grad_pair_two = jnp.concatenate([grad_k_two, grad_v_two], axis=-1)
    grad_query_cross = weight_grad(normed_two, grad_q_two)
    grad_pair_cross = weight_grad(encoder_all, grad_pair_two)
    folded_two = ctx_fold(grad_pair_two, 1, False).astype(jnp.bfloat16)
    grad_states = pair_total(mm_back(folded_two, pair_cross))
    grad_from, grad_gain_cross = rms_backward(grad_normed, unit_two, inverse_two, gain_cross)
    grad_res = grad_res + grad_from

    grad_low = grad_res.astype(jnp.bfloat16)
    grad_attended = mm(grad_low, output_self).astype(jnp.bfloat16)
    grad_out_self = weight_grad(grad_low, attended_one)
    grads_middle = scatter_rows(
        jnp.concatenate([grad_query_cross, grad_pair_cross, grad_out_self, grad_out_cross], axis=1)
    )
    grad_q_one, grad_k_one, grad_v_one, line_grads = attend_backward(
        queries_one, pair_one, query_docs, dec_docs, attended_one, logs_one, grad_attended,
        place, lines,
    )
    grad_pair_one = jnp.concatenate([grad_k_one, grad_v_one], axis=-1)
    folded_one = ctx_fold(grad_pair_one, 1, True).astype(jnp.bfloat16)
    grads_self = scatter_rows(
        jnp.concatenate(
            [weight_grad(normed_one, grad_q_one), weight_grad(normed_all, grad_pair_one)], axis=1
        )
    )
    grad_normed = pair_total(
        mm_back(grad_q_one, query_self) + mm_back(folded_one, pair_self)
    )
    grad_from, grad_gain_self = rms_backward(grad_normed, unit_one, inverse_one, gain_self)
    grad_input = (grad_res + grad_from).astype(jnp.bfloat16)

    line_grads = line_grads[:, :2].reshape(head_count, row_count + length)
    spread = lax.dynamic_update_slice_in_dim(
        jnp.zeros((head_count, 2 * length), jnp.float32), line_grads, offset, 1
    )[:, length:]
    grad_bias = jnp.dot(spread, bucket_onehot, precision=lax.Precision.HIGHEST).T
    totals = jnp.concatenate(
        [grad_gain_self, grad_gain_cross, grad_gain_ffn, grad_bias.reshape(-1)]
    )
    totals = lax.psum(totals, ("fsdp", "ctx"))
    shard = lax.axis_index("fsdp")
    gain_grads = [
        lax.dynamic_slice_in_dim(totals, width * i + shard * gain_rows, gain_rows, 0)
        for i in range(3)
    ]
    bias_grad = lax.dynamic_slice_in_dim(
        totals, 3 * width + shard * bucket_rows * head_count, bucket_rows * head_count, 0
    ).reshape(bucket_rows, head_count)
    hw = heads_width
    return (
        layer_output.astype(jnp.bfloat16),
        grad_input,
        grad_states.astype(jnp.bfloat16),
        gain_grads[0],
        grads_self[:, :hw],
        grads_self[:, hw : 2 * hw],
        grads_self[:, 2 * hw :],
        grads_middle[:, 3 * hw : 4 * hw].T,
        bias_grad,
        gain_grads[1],
        grads_middle[:, :hw],
        grads_middle[:, hw : 2 * hw],
        grads_middle[:, 2 * hw : 3 * hw],
        grads_middle[:, 4 * hw :].T,
        gain_grads[2],
        grads_ffn[:, :units],
        grads_ffn[:, units : 2 * units],
        grads_ffn[:, 2 * units :].T,
    )


def solution(mesh):
    in_specs = (
        P("fsdp", "ctx", None),
        P("fsdp", "ctx", None),
        P("fsdp", None),
        P("fsdp", None),
        P(),
        P("fsdp", "ctx", None),
        P("fsdp"),
        P("fsdp", "tp"),
        P("fsdp", "tp"),
        P("fsdp", "tp"),
        P("tp", "fsdp"),
        P("fsdp", "tp"),
        P("fsdp"),
        P("fsdp", "tp"),
        P("fsdp", "tp"),
        P("fsdp", "tp"),
        P("tp", "fsdp"),
        P("fsdp"),
        P("fsdp", "tp"),
        P("fsdp", "tp"),
        P("tp", "fsdp"),
    )
    out_specs = (
        P("fsdp", "ctx", None),
        P("fsdp", "ctx", None),
        P("fsdp", "ctx", None),
        P("fsdp"),
        P("fsdp", "tp"),
        P("fsdp", "tp"),
        P("fsdp", "tp"),
        P("tp", "fsdp"),
        P("fsdp", "tp"),
        P("fsdp"),
        P("fsdp", "tp"),
        P("fsdp", "tp"),
        P("fsdp", "tp"),
        P("tp", "fsdp"),
        P("fsdp"),
        P("fsdp", "tp"),
        P("fsdp", "tp"),
        P("tp", "fsdp"),
    )
    return jax.shard_map(body, mesh=mesh, in_specs=in_specs, out_specs=out_specs, check_vma=False)
```

```python
import functools
import jax
import jax.numpy as jnp
from jax import lax
from jax.experimental import pallas as pl
from jax.experimental.pallas import tpu as pltpu
from jax.sharding import PartitionSpec as P

EPSILON = 1e-06
NEGATIVE = -1e30
EXTRA = 16
TINY = pl.CostEstimate(flops=1, bytes_accessed=1, transcendentals=0)
LANES = 128
CHUNK = 256
NT = (((1,), (1,)), ((), ()))
NN = (((1,), (0,)), ((), ()))


def dot(lhs, rhs, dims=NN):
    return lax.dot_general(lhs, rhs, dims, preferred_element_type=jnp.float32)


def fill_mask(mask_ref, seg_row, seg_col_ref, offset_ref, causal):
    rows = seg_row.shape[1]
    keys = mask_ref.shape[0]
    for start in range(0, keys, CHUNK):
        size = min(CHUNK, keys - start)
        seen = seg_col_ref[0, pl.ds(start, size), :] == seg_row
        if causal:
            key_place = lax.broadcasted_iota(jnp.int32, (size, rows), 0) + start
            query_place = lax.broadcasted_iota(jnp.int32, (size, rows), 1) + offset_ref[0, 0]
            seen = seen & (key_place <= query_place)
        mask_ref[pl.ds(start, size), :] = jnp.where(seen, 0.0, NEGATIVE)


def fill_bias(bias_ref, head, line):
    width = line.shape[1]
    base = jnp.broadcast_to(line, (8, width))
    row = lax.broadcasted_iota(jnp.int32, (8, width), 0)
    for bit in (1, 2, 4):
        base = jnp.where((row & bit) != 0, pltpu.roll(base, bit, 1), base)
    for block in range(LANES // 8):
        bias_ref[head, pl.ds(8 * block, 8), :] = pltpu.roll(base, 8 * block, 1) if block else base


def fold_diagonals(total):
    width = total.shape[1]
    half = total.shape[0] // 2
    while half >= 8:
        total = total[:half] + pltpu.roll(total[half:], width - half, 1)
        half //= 2
    row = lax.broadcasted_iota(jnp.int32, (8, width), 0)
    for bit in (4, 2, 1):
        total = jnp.where((row & bit) != 0, pltpu.roll(total, width - bit, 1), total)
    return jnp.sum(total, axis=0, keepdims=True)


def head_mask(rows, head):
    lane = lax.broadcasted_iota(jnp.int32, (rows, LANES), 1)
    return (lane // (LANES // 2)) == head


def add_bias(scores, bias_ref, head, start, keys, rows):
    parts = []
    for sub in range(0, scores.shape[0], LANES):
        at = keys - (start + sub)
        parts.append(scores[sub : sub + LANES] + bias_ref[head, :, at : at + rows])
    return jnp.concatenate(parts, axis=0)


def forward_kernel(causal, *refs):
    if causal:
        (offset_ref, line_ref, seg_row_ref, seg_col_ref, q_ref, k_ref, v_ref, out_ref, log_ref,
         mask_ref, score_ref, bias_ref) = refs
    else:
        (seg_row_ref, seg_col_ref, q_ref, k_ref, v_ref, out_ref, log_ref,
         mask_ref, score_ref) = refs
        offset_ref = None
    pair = pl.program_id(0)
    seq = pl.program_id(1)
    rows = q_ref.shape[1]
    keys = k_ref.shape[1]

    @pl.when(pair == 0)
    def _():
        fill_mask(mask_ref.at[seq], seg_row_ref[0], seg_col_ref, offset_ref, causal)

    if causal:

        @pl.when(seq == 0)
        def _():
            for head in range(2):
                fill_bias(bias_ref, head, line_ref[0, pl.ds(head, 1), :])

    q = q_ref[0]
    v_turned = v_ref[0].T
    half = LANES // 2
    outs = []
    logs = []
    for head in range(2):
        q_head = jnp.where(head_mask(rows, head), q, jnp.zeros_like(q))
        highest = None
        for start in range(0, keys, CHUNK):
            scores = dot(k_ref[0, pl.ds(start, CHUNK), :], q_head, NT)
            scores = scores + mask_ref[seq, pl.ds(start, CHUNK), :]
            if causal:
                scores = add_bias(scores, bias_ref, head, start, keys, rows)
            score_ref[pl.ds(start, CHUNK), :] = scores
            top = jnp.max(scores, axis=0, keepdims=True)
            highest = top if highest is None else jnp.maximum(highest, top)
        total = None
        attended = None
        for start in range(0, keys, CHUNK):
            grown = jnp.exp(score_ref[pl.ds(start, CHUNK), :] - highest)
            part = jnp.sum(grown, axis=0, keepdims=True)
            piece = dot(v_turned[half * head : half * head + half, start : start + CHUNK],
                        grown.astype(jnp.bfloat16))
            total = part if total is None else total + part
            attended = piece if attended is None else attended + piece
        outs.append(attended / total)
        logs.append(highest + jnp.log(total))
    out_ref[0] = jnp.concatenate(outs, axis=0).T.astype(jnp.bfloat16)
    log_ref[0, 0] = jnp.concatenate(logs + [jnp.zeros((6, rows), jnp.float32)], axis=0)


def backward_kernel(causal, *refs):
    if causal:
        (offset_ref, line_ref, seg_row_ref, seg_col_ref, q_ref, k_ref, v_ref, out_ref, log_ref,
         grad_ref, dq_ref, dk_ref, dv_ref, line_grad_ref, mask_ref, bias_ref, total_ref) = refs
    else:
        (seg_row_ref, seg_col_ref, q_ref, k_ref, v_ref, out_ref, log_ref,
         grad_ref, dq_ref, dk_ref, dv_ref, mask_ref) = refs
        offset_ref = None
    pair = pl.program_id(0)
    seq = pl.program_id(1)
    rows = q_ref.shape[1]
    keys = k_ref.shape[1]
    half = LANES // 2

    @pl.when(pair == 0)
    def _():
        fill_mask(mask_ref.at[seq], seg_row_ref[0], seg_col_ref, offset_ref, causal)

    if causal:

        @pl.when(seq == 0)
        def _():
            for head in range(2):
                fill_bias(bias_ref, head, line_ref[0, pl.ds(head, 1), :])
            total_ref[...] = jnp.zeros_like(total_ref)

    q = q_ref[0]
    grad = grad_ref[0]
    product = grad.astype(jnp.float32) * out_ref[0].astype(jnp.float32)
    chooser = (
        lax.broadcasted_iota(jnp.int32, (8, LANES), 1) // half
        == lax.broadcasted_iota(jnp.int32, (8, LANES), 0)
    ).astype(jnp.float32)
    inner = lax.dot_general(chooser, product, NT, precision=lax.Precision.HIGHEST,
                            preferred_element_type=jnp.float32)
    q_heads = [jnp.where(head_mask(rows, h), q, jnp.zeros_like(q)) for h in range(2)]
    grad_heads = [jnp.where(head_mask(rows, h), grad, jnp.zeros_like(grad)) for h in range(2)]
    dq = [None, None]
    for start in range(0, keys, CHUNK):
        k = k_ref[0, pl.ds(start, CHUNK), :]
        v = v_ref[0, pl.ds(start, CHUNK), :]
        k_turned = k.T
        dk = None
        dv = None
        for head in range(2):
            scores = dot(k, q_heads[head], NT)
            scores = scores + mask_ref[seq, pl.ds(start, CHUNK), :]
            if causal:
                scores = add_bias(scores, bias_ref, head, start, keys, rows)
            weights = jnp.exp(scores - log_ref[0, 0, pl.ds(head, 1), :])
            dv_part = dot(weights.astype(jnp.bfloat16), grad_heads[head])
            dw = dot(v, grad_heads[head], NT)
            ds = weights * (dw - inner[head : head + 1])
            ds_low = ds.astype(jnp.bfloat16)
            dk_part = dot(ds_low, q_heads[head])
            dq_part = dot(k_turned[half * head : half * head + half], ds_low)
            dv = dv_part if dv is None else dv + dv_part
            dk = dk_part if dk is None else dk + dk_part
            dq[head] = dq_part if dq[head] is None else dq[head] + dq_part
            if causal:
                for sub in range(0, CHUNK, LANES):
                    at = keys - (start + sub)
                    total_ref[head, :, at : at + rows] += ds[sub : sub + LANES]
        dk_ref[0, pl.ds(start, CHUNK), :] = dk.astype(jnp.bfloat16)
        dv_ref[0, pl.ds(start, CHUNK), :] = dv.astype(jnp.bfloat16)
    dq_ref[0] = jnp.concatenate(dq, axis=0).T.astype(jnp.bfloat16)
    if causal:

        @pl.when(seq == pl.num_programs(1) - 1)
        def _():
            lines = [fold_diagonals(total_ref[head]) for head in range(2)]
            lines.append(jnp.zeros((6, lines[0].shape[1]), jnp.float32))
            line_grad_ref[0] = jnp.concatenate(lines, axis=0)


def specs_for(rows, keys, pairs, causal):
    def wide(count, shift=0):
        return pl.BlockSpec((1, count, LANES), lambda p, s: (s, 0, p + shift))

    lead = []
    if causal:
        lead = [
            pl.BlockSpec((1, 1), lambda p, s: (0, 0), memory_space=pltpu.SMEM),
            pl.BlockSpec((1, 8, rows + keys), lambda p, s: (p, 0, 0)),
        ]
    lead += [
        pl.BlockSpec((1, 1, rows), lambda p, s: (s, 0, 0)),
        pl.BlockSpec((1, keys, 1), lambda p, s: (s, 0, 0)),
        wide(rows),
        wide(keys),
        wide(keys, pairs),
    ]
    return lead, wide, pl.BlockSpec((1, 1, 8, rows), lambda p, s: (s, p, 0, 0))


def attend_forward(q, kv, seg_row, seg_col, offset=None, lines=None):
    seqs, rows, width = q.shape
    keys = kv.shape[1]
    pairs = width // LANES
    causal = lines is not None
    lead, wide, logs = specs_for(rows, keys, pairs, causal)
    scratch = [pltpu.VMEM((seqs, keys, rows), jnp.float32), pltpu.VMEM((keys, rows), jnp.float32)]
    args = [seg_row, seg_col, q, kv, kv]
    if causal:
        args = [offset, lines] + args
        scratch.append(pltpu.VMEM((2, LANES, rows + keys), jnp.float32))
    return pl.pallas_call(
        functools.partial(forward_kernel, causal),
        grid=(pairs, seqs),
        in_specs=lead,
        out_specs=[wide(rows), logs],
        out_shape=[
            jax.ShapeDtypeStruct((seqs, rows, width), jnp.bfloat16),
            jax.ShapeDtypeStruct((seqs, pairs, 8, rows), jnp.float32),
        ],
        scratch_shapes=scratch,
        compiler_params=pltpu.CompilerParams(vmem_limit_bytes=40 * 1024 * 1024),
        cost_estimate=TINY,
        name="attend_forward",
    )(*args)


def attend_backward(q, kv, seg_row, seg_col, out, logs_value, grad, offset=None, lines=None):
    seqs, rows, width = q.shape
    keys = kv.shape[1]
    pairs = width // LANES
    causal = lines is not None
    lead, wide, logs = specs_for(rows, keys, pairs, causal)
    scratch = [pltpu.VMEM((seqs, keys, rows), jnp.float32)]
    args = [seg_row, seg_col, q, kv, kv, out, logs_value, grad]
    out_shape = [
        jax.ShapeDtypeStruct((seqs, rows, width), jnp.bfloat16),
        jax.ShapeDtypeStruct((seqs, keys, width), jnp.bfloat16),
        jax.ShapeDtypeStruct((seqs, keys, width), jnp.bfloat16),
    ]
    out_specs = [wide(rows), wide(keys), wide(keys)]
    if causal:
        args = [offset, lines] + args
        scratch.append(pltpu.VMEM((2, LANES, rows + keys), jnp.float32))
        scratch.append(pltpu.VMEM((2, LANES, rows + keys), jnp.float32))
        out_shape.append(jax.ShapeDtypeStruct((pairs, 8, rows + keys), jnp.float32))
        out_specs.append(pl.BlockSpec((1, 8, rows + keys), lambda p, s: (p, 0, 0)))
    return pl.pallas_call(
        functools.partial(backward_kernel, causal),
        grid=(pairs, seqs),
        in_specs=lead + [wide(rows), logs, wide(rows)],
        out_specs=out_specs,
        out_shape=out_shape,
        scratch_shapes=scratch,
        compiler_params=pltpu.CompilerParams(vmem_limit_bytes=40 * 1024 * 1024),
        cost_estimate=TINY,
        name="attend_backward",
    )(*args)


def gradient_kernel(spans, tokens, split, *refs):
    if split:
        place_ref, refs = refs[0], refs[1:]
    lhs_count = len(tokens)
    lhs_refs = refs[:lhs_count]
    seqs = (len(refs) - lhs_count - (3 if split else 2)) // len(spans)
    rhs_refs = refs[lhs_count : lhs_count + seqs * len(spans)]
    outs = refs[lhs_count + seqs * len(spans) : -1]
    turned_ref = refs[-1]
    step = pl.program_id(0)
    for index, (first, last, group) in enumerate(spans):

        @pl.when(step == first)
        def _():
            if index == 0 or spans[index - 1][2] != group:
                for s in range(seqs):
                    lhs = lhs_refs[group * seqs + s]
                    size = lhs.shape[0]
                    turned_ref[:, s * size : (s + 1) * size] = lhs[...].T

        @pl.when((step >= first) & (step < last))
        def _():
            total = None
            for s in range(seqs):
                size = lhs_refs[group * seqs + s].shape[0]
                part = dot(turned_ref[:, s * size : (s + 1) * size], rhs_refs[index * seqs + s][...])
                total = part if total is None else total + part
            if split:
                low = place_ref[0, 0]
                rows = split
                for block in range(total.shape[0] // (2 * rows)):
                    even = total[2 * block * rows : (2 * block + 1) * rows]
                    odd = total[(2 * block + 1) * rows : (2 * block + 2) * rows]
                    at = pl.ds(block * rows, rows)
                    outs[0][at, :] = jnp.where(low == 0, odd, even).astype(jnp.bfloat16)
                    outs[1][at, :] = jnp.where(low == 0, even, odd).astype(jnp.bfloat16)
            else:
                outs[0][...] = total.astype(jnp.bfloat16)


def gradient_blocks(segments, columns, place=None, split=0):
    width = segments[0][0][0].shape[1]
    lhs_args, lhs_keys, rhs_args, rhs_specs, spans, specs = [], [], [], [], [], []
    first = 0
    flops = 0
    for lhs, rhs in segments:
        count = rhs[0].shape[1] // columns
        key = tuple(id(v) for v in lhs)
        if key not in lhs_keys:
            lhs_keys.append(key)
            lhs_args.extend(lhs)
        spans.append((first, first + count, lhs_keys.index(key)))
        for value in rhs:
            flops += 2 * value.shape[0] * value.shape[1] * width

            def where(i, first=first, count=count):
                return (0, jnp.clip(i - first, 0, count - 1))

            rhs_args.append(value)
            rhs_specs.append(pl.BlockSpec((value.shape[0], columns), where))
        first += count
    for value in lhs_args:
        specs.append(pl.BlockSpec(value.shape, lambda i: (0, 0)))
    tokens = [v.shape[0] for v in lhs_args]
    longest = max(sum(v.shape[0] for v in lhs) for lhs, rhs in segments)
    out_width = first * columns
    args = lhs_args + rhs_args
    specs = specs + rhs_specs
    if split:
        args = [place] + args
        specs = [pl.BlockSpec((1, 1), lambda i: (0, 0), memory_space=pltpu.SMEM)] + specs
        shapes = [jax.ShapeDtypeStruct((width // 2, out_width), jnp.bfloat16)] * 2
        out_specs = [pl.BlockSpec((width // 2, columns), lambda i: (0, i))] * 2
    else:
        shapes = jax.ShapeDtypeStruct((width, out_width), jnp.bfloat16)
        out_specs = pl.BlockSpec((width, columns), lambda i: (0, i))
    return pl.pallas_call(
        functools.partial(gradient_kernel, spans, tokens, split),
        grid=(first,),
        in_specs=specs,
        out_specs=out_specs,
        out_shape=shapes,
        scratch_shapes=[pltpu.VMEM((width, longest), jnp.bfloat16)],
        compiler_params=pltpu.CompilerParams(vmem_limit_bytes=48 * 1024 * 1024),
        cost_estimate=TINY,
        name="weight_gradients",
    )(*args)


def mm(lhs, rhs):
    return dot(lhs, rhs)


def mm_back(lhs, rhs):
    return dot(lhs, rhs, NT)


def rms_forward(values, gain_row):
    inverse_rms = lax.rsqrt(jnp.mean(values * values, axis=-1, keepdims=True) + EPSILON)
    unit_rows = values * inverse_rms
    return unit_rows, inverse_rms, (unit_rows * gain_row).astype(jnp.bfloat16)


def rms_backward(grad_normed, unit_rows, inverse_rms, gain_row):
    grad_unit = grad_normed * gain_row
    grad_gain = jnp.sum(grad_normed * unit_rows, axis=0)
    inner_sum = jnp.mean(grad_unit * unit_rows, axis=-1, keepdims=True)
    return inverse_rms * (grad_unit - unit_rows * inner_sum), grad_gain


def low_cast(value):
    return value.astype(jnp.bfloat16)


def wide_cast(value):
    return value.astype(jnp.float32)


def ctx_shape():
    count = lax.axis_size("ctx")
    low = 2 if count % 2 == 0 else 1
    return count // low, low


def ctx_place():
    high, low = ctx_shape()
    index = lax.axis_index("ctx")
    return index // low, index % low


def swap_low(value):
    high, low = ctx_shape()
    return lax.ppermute(value, "ctx", [(i, i ^ 1) for i in range(high * low)])


def shift_high(value, step, wrap):
    high, low = ctx_shape()
    pairs = []
    for i in range(high * low):
        target = i // low + step
        if wrap or 0 <= target < high:
            pairs.append((i, (target % high) * low + i % low))
    return lax.ppermute(value, "ctx", pairs)


def shift_fsdp(value, step):
    count = lax.axis_size("fsdp")
    return lax.ppermute(value, "fsdp", [(i, (i + step) % count) for i in range(count)])


def put(buffer, value, at, axis):
    return lax.dynamic_update_slice_in_dim(buffer, jnp.expand_dims(value, axis), at, axis)


def ctx_gather(value, causal, axis, earlier):
    high, low = ctx_shape()
    at_high, at_low = ctx_place()
    pieces = [value] + [shift_high(value, step, not causal) for step in range(1, high)]
    pieces = before(pieces, earlier)
    places = [((at_high - step) % high, at_low) for step in range(high)]
    if low == 2:
        pieces = pieces + [swap_low(piece) for piece in pieces]
        places = places + [((at_high - step) % high, 1 - at_low) for step in range(high)]
    shape = value.shape[:axis] + (high, low) + value.shape[axis:]
    held = assemble(pieces, places, shape, axis)
    shape = value.shape[:axis] + (high * low * value.shape[axis],) + value.shape[axis + 1 :]
    return held.reshape(shape)


def gather_rows(shards, earlier):
    count = lax.axis_size("ctx")
    rows = shards[0].shape[0] // count
    start = lax.axis_index("ctx") * rows
    shards = before(shards, earlier)
    parts = [lax.dynamic_slice_in_dim(s, start, rows, 0) for s in shards]
    part = jnp.concatenate(parts, axis=1) if len(parts) > 1 else parts[0]
    return lax.all_gather(part, ("fsdp", "ctx"), axis=0, tiled=True)


def before(value, *earlier):
    return lax.optimization_barrier((value, earlier))[0]


def assemble_kernel(lead, place_ref, *refs):
    pieces, out_ref = refs[:-1], refs[-1]
    step = pl.program_id(0)
    for index, piece in enumerate(pieces):

        @pl.when(step == index)
        def _():
            rows = out_ref.shape[-2]
            out_ref[...] = piece[..., :rows, :].reshape(out_ref.shape)


def assemble(pieces, places, shape, lead):
    places = jnp.stack([jnp.stack([jnp.asarray(v, jnp.int32) for v in p]) for p in places])
    block = shape[:lead] + (1, 1) + shape[lead + 2 :]
    rank = len(pieces[0].shape)

    def where(i, place):
        return (0,) * lead + (place[i, 0], place[i, 1]) + (0,) * (len(shape) - lead - 2)

    return pl.pallas_call(
        functools.partial(assemble_kernel, lead),
        grid_spec=pltpu.PrefetchScalarGridSpec(
            num_scalar_prefetch=1,
            grid=(len(pieces),),
            in_specs=[pl.BlockSpec(p.shape, lambda i, place: (0,) * rank) for p in pieces],
            out_specs=pl.BlockSpec(block, where),
        ),
        out_shape=jax.ShapeDtypeStruct(shape, pieces[0].dtype),
        compiler_params=pltpu.CompilerParams(vmem_limit_bytes=40 * 1024 * 1024),
        cost_estimate=TINY,
        name="assemble",
    )(places, *pieces)


def first_part(shards):
    high, low = ctx_shape()
    at_high, at_low = ctx_place()
    rows = shards[0].shape[0] // low
    parts = [lax.dynamic_slice_in_dim(s, at_low * rows, rows, 0) for s in shards]
    return jnp.concatenate(parts, axis=1) if len(parts) > 1 else parts[0]


def first_pieces(part):
    count = lax.axis_size("fsdp")
    if count > 8:
        held = lax.all_gather(part, "fsdp", axis=0, tiled=False)
        index = lax.axis_index("fsdp")
        return [
            lax.dynamic_index_in_dim(held, (index - step) % count, 0, False)
            for step in range(count)
        ]
    return [part] + [shift_fsdp(part, step) for step in range(1, count)]


def first_whole(pieces, rows):
    count = lax.axis_size("fsdp")
    index = lax.axis_index("fsdp")
    high, low = ctx_shape()
    at_high, at_low = ctx_place()
    columns = pieces[0].shape[1]
    places = [((index - step) % count, at_low) for step in range(count)]
    if low == 2:
        pieces = pieces + [swap_low(piece) for piece in pieces]
        places = places + [((index - step) % count, 1 - at_low) for step in range(count)]
    whole = assemble(pieces, places, (count, low, rows, columns), 0)
    return whole.reshape(count * low * rows, columns)


def gather_small(value):
    count = lax.axis_size("fsdp")
    index = lax.axis_index("fsdp")
    if count > 8:
        return lax.all_gather(value, "fsdp", axis=0, tiled=False)
    held = put(jnp.zeros((count,) + value.shape, value.dtype), value, index, 0)
    for step in range(1, count):
        held = put(held, shift_fsdp(value, step), (index - step) % count, 0)
    return held


def fold_start(segments, columns):
    high, low = ctx_shape()
    at_high, at_low = ctx_place()
    count = lax.axis_size("fsdp")
    width = segments[0][0][0].shape[1]
    rows = width // (count * high * low)
    shape = (count, high, rows, -1)
    if low == 2:
        place = jnp.full((1, 1), at_low, jnp.int32)
        away, kept = gradient_blocks(segments, columns, place, rows)
        return [kept.reshape(shape), swap_low(away).reshape(shape)], away
    kept = gradient_blocks(segments, columns)
    return [kept.reshape(shape)], kept


def fold_high(halves, earlier=()):
    high, low = ctx_shape()
    at_high, at_low = ctx_place()
    halves = before(halves, earlier)

    def part(at):
        return low_cast(sum(wide_cast(lax.dynamic_index_in_dim(h, at, 1, False)) for h in halves))

    sent = [part((at_high + step) % high) for step in range(1, high)]
    mine = part(at_high)
    moved = [shift_high(piece, step + 1, True) for step, piece in enumerate(sent)]
    return [mine] + moved, (mine, sent)


def fold_fsdp(parts, lines, earlier=()):
    count = lax.axis_size("fsdp")
    index = lax.axis_index("fsdp")
    parts, lines = before((parts, lines), earlier)
    small = jnp.zeros((count, EXTRA, parts[0].shape[2]), jnp.bfloat16)
    small = small.at[:, 0, : lines.shape[1]].set(low_cast(lines))
    if count > 8:
        whole = low_cast(sum(wide_cast(p) for p in parts))
        whole = jnp.concatenate([whole, small], axis=1)
        flat = whole.reshape((-1,) + whole.shape[2:])
        return [lax.psum_scatter(flat, "fsdp", scatter_dimension=0, tiled=True)], whole

    def part(at):
        total = sum(wide_cast(lax.dynamic_index_in_dim(p, at, 0, False)) for p in parts)
        line = lax.dynamic_index_in_dim(small, at, 0, False)
        return jnp.concatenate([low_cast(total), line], axis=0)

    sent = [part((index + step) % count) for step in range(1, count)]
    mine = part(index)
    moved = [shift_fsdp(piece, step + 1) for step, piece in enumerate(sent)]
    return [mine] + moved, (mine, sent)


def fold_fsdp_first(halves, earlier=()):
    count = lax.axis_size("fsdp")
    index = lax.axis_index("fsdp")
    halves = before(halves, earlier)
    if count > 8:
        whole = low_cast(sum(wide_cast(h) for h in halves))
        flat = whole.reshape((-1,) + whole.shape[2:])
        part = lax.psum_scatter(flat, "fsdp", scatter_dimension=0, tiled=True)
        return [part.reshape(whole.shape[1:])], whole

    def part(at):
        return low_cast(sum(wide_cast(lax.dynamic_index_in_dim(h, at, 0, False)) for h in halves))

    sent = [part((index + step) % count) for step in range(1, count)]
    mine = part(index)
    moved = [shift_fsdp(piece, step + 1) for step, piece in enumerate(sent)]
    return [mine] + moved, (mine, sent)


def fold_high_last(parts, earlier=()):
    high, low = ctx_shape()
    at_high, at_low = ctx_place()
    parts = before(parts, earlier)

    def part(at):
        return low_cast(sum(wide_cast(lax.dynamic_index_in_dim(p, at, 0, False)) for p in parts))

    sent = [part((at_high + step) % high) for step in range(1, high)]
    mine = part(at_high)
    moved = [shift_high(piece, step + 1, True) for step, piece in enumerate(sent)]
    return [mine] + moved, (mine, sent)


def fold_own(parts, earlier=()):
    parts = before(parts, earlier)
    return low_cast(sum(wide_cast(p) for p in parts))


def spread_high(part):
    high, low = ctx_shape()
    return [part] + [shift_high(part, step, True) for step in range(1, high)]


def spread_low(parts, earlier=()):
    high, low = ctx_shape()
    held = jnp.stack(before(parts, earlier))
    return [held, swap_low(held) if low == 2 else held], held


def finish_kernel(high, low, cuts, extra, place_ref, mine_ref, other_ref, *outs):
    rows = mine_ref.shape[1] - extra
    for (start, stop, turned), out in zip(cuts, outs):
        blocks = []
        for at_high in range(high):
            step = lax.rem(place_ref[0, 0] - at_high + high, high)
            for at_low in range(low):
                mine = mine_ref[step, :rows, start:stop]
                other = other_ref[step, :rows, start:stop]
                chosen = jnp.where(place_ref[0, 1] == at_low, mine, other)
                blocks.append(chosen.astype(jnp.float32))
        whole = jnp.concatenate(blocks, axis=0)
        out[...] = whole.T if turned else whole
    if extra:
        total = None
        for step in range(high):
            for ref in (mine_ref, other_ref)[:low]:
                line = ref[step, rows:, :].astype(jnp.float32)
                total = line if total is None else total + line
        outs[-1][...] = total


def spread_end(pair, cuts, extra=0, earlier=()):
    high, low = ctx_shape()
    at_high, at_low = ctx_place()
    mine, other = before(pair, earlier)
    rows = mine.shape[1] - extra
    shapes = []
    for start, stop, turned in cuts:
        shape = (high * low * rows, stop - start)
        shapes.append(jax.ShapeDtypeStruct(shape[::-1] if turned else shape, jnp.float32))
    if extra:
        shapes.append(jax.ShapeDtypeStruct((extra, mine.shape[2]), jnp.float32))
    place = jnp.stack([at_high, at_low]).astype(jnp.int32).reshape(1, 2)
    whole = pl.BlockSpec(memory_space=pltpu.VMEM)
    return pl.pallas_call(
        functools.partial(finish_kernel, high, low, cuts, extra),
        in_specs=[pl.BlockSpec(memory_space=pltpu.SMEM), whole, whole],
        out_specs=[whole] * len(shapes),
        out_shape=shapes,
        compiler_params=pltpu.CompilerParams(vmem_limit_bytes=48 * 1024 * 1024),
        cost_estimate=TINY,
        name="finish",
    )(place, mine, other)


def block_fold_start(lefts, rights):
    high, low = ctx_shape()
    at_high, at_low = ctx_place()
    size = lefts[0].shape[0] // (high * low)

    def part(at):
        views = [v.reshape(high, low, size, -1) for v in lefts + rights]
        views = [lax.dynamic_index_in_dim(v, at, 1, False) for v in views]
        views = [
            jnp.concatenate([views[i], views[len(lefts) + i]], axis=-1) for i in range(len(lefts))
        ]
        return jnp.concatenate(views, axis=1) if len(views) > 1 else views[0]

    if low == 1:
        whole = part(0)
        return [whole], whole
    away = part(1 - at_low)
    kept = part(at_low)
    return [kept, swap_low(away)], (kept, away)


def block_fold_high(halves, causal, earlier=()):
    high, low = ctx_shape()
    at_high, at_low = ctx_place()
    halves = before(halves, earlier)

    def part(at):
        return low_cast(sum(wide_cast(lax.dynamic_index_in_dim(h, at, 0, False)) for h in halves))

    sent = [part((at_high - step) % high) for step in range(1, high)]
    mine = part(at_high)
    moved = [shift_high(piece, -step - 1, not causal) for step, piece in enumerate(sent)]
    return [mine] + moved, (mine, sent)


def block_fold_end(parts, earlier=()):
    parts = before(parts, earlier)
    return low_cast(sum(wide_cast(p) for p in parts))


def pair_start(partial):
    own = low_cast(partial)
    count = lax.axis_size("tp")
    moved = [
        lax.ppermute(own, "tp", [(i, (i + step) % count) for i in range(count)])
        for step in range(1, count)
    ]
    return [own] + moved, own


def pair_end(parts, earlier=()):
    parts = before(parts, earlier)
    return sum(wide_cast(p) for p in parts)


def body(
    hidden_in,
    encoder_states,
    dec_segments,
    enc_segments,
    bucket_table,
    out_cotangent,
    self_gain,
    self_query,
    self_key,
    self_value,
    self_output,
    position_bias,
    cross_gain,
    cross_query,
    cross_key,
    cross_value,
    cross_output,
    ffn_gain,
    ffn_gate,
    ffn_up,
    ffn_down,
):
    shards = lax.axis_size("fsdp")
    seqs, row_count, width = hidden_in.shape
    length = dec_segments.shape[1]
    hw = self_query.shape[1]
    units = ffn_gate.shape[1]
    bucket_rows, head_count = position_bias.shape
    bucket_count = bucket_rows * shards
    gain_rows = self_gain.shape[0]
    offset = lax.axis_index("ctx") * row_count
    every = range(seqs)

    small = jnp.concatenate([self_gain, cross_gain, ffn_gain, position_bias.reshape(-1)])
    line = jnp.zeros((EXTRA, 3 * hw), jnp.bfloat16).at[0, : small.shape[0]].set(small)
    qkv_part = first_part([self_query, self_key, self_value])
    first_rows = qkv_part.shape[0]
    qkv_part = jnp.concatenate([qkv_part, line], axis=0)
    first_arrived = first_pieces(qkv_part)
    shard = lax.axis_index("fsdp")
    small = jnp.stack([piece[first_rows, : small.shape[0]] for piece in first_arrived])
    small = jnp.stack(
        [lax.dynamic_index_in_dim(small, (shard - i) % shards, 0, False) for i in range(shards)]
    )
    gain_self, gain_cross, gain_ffn = [
        wide_cast(small[:, gain_rows * i : gain_rows * (i + 1)].reshape(width)) for i in range(3)
    ]
    bias_table = wide_cast(small[:, 3 * gain_rows :].reshape(bucket_count, head_count))
    first_weights = first_whole(first_arrived, first_rows)
    hidden_all = ctx_gather(before(hidden_in, qkv_part), True, 1, first_arrived[-1])
    source = [wide_cast(hidden_in[s]) for s in every]
    norm_one = [rms_forward(source[s], gain_self) for s in every]
    norm_all = [rms_forward(wide_cast(hidden_all[s]), gain_self)[2] for s in every]
    middle_weights = gather_rows(
        [self_output.T, cross_query, cross_key, cross_value, cross_output.T], qkv_part
    )
    gate_up = gather_rows([ffn_gate, ffn_up], qkv_part)
    ffn_down, encoder_states = before((ffn_down, encoder_states), first_weights, norm_all[0])
    down_pieces = first_pieces(first_part([ffn_down.T]))
    query_self = first_weights[:, :hw]
    pair_self = first_weights[:, hw:]
    output_self = middle_weights[:, :hw]
    query_cross = middle_weights[:, hw : 2 * hw]
    pair_cross = middle_weights[:, 2 * hw : 4 * hw]
    output_cross = middle_weights[:, 4 * hw :]

    query_docs = lax.dynamic_slice_in_dim(dec_segments, offset, row_count, 1)[:, None, :]
    dec_docs = dec_segments[:, :, None]
    enc_docs = enc_segments[:, :, None]
    bucket_onehot = wide_cast(
        bucket_table[:, None] == jnp.arange(bucket_count, dtype=jnp.int32)[None, :]
    )
    distance_bias = jnp.dot(bucket_onehot, bias_table, precision=lax.Precision.HIGHEST).T
    padded = jnp.concatenate([jnp.zeros_like(distance_bias), distance_bias], axis=1)
    lines = lax.dynamic_slice_in_dim(padded, offset, row_count + length, 1)
    lines = lines.reshape(head_count // 2, 2, row_count + length)
    lines = jnp.concatenate(
        [lines, jnp.zeros((head_count // 2, 6, row_count + length), jnp.float32)], axis=1
    )
    place = jnp.full((1, 1), offset, jnp.int32)

    def one(value, s):
        return value[s : s + 1]

    q_one, kv_one, att_one, log_one, pair_one, done = [], [], [], [], [], ()
    for s in every:
        rows_all, rows_own = before((norm_all[s], norm_one[s][2]), done)
        kv_one.append(low_cast(mm(rows_all, pair_self)))
        q_one.append(low_cast(mm(rows_own, query_self)))
        out, logs = attend_forward(
            q_one[s][None], kv_one[s][None], one(query_docs, s), one(dec_docs, s), place, lines
        )
        att_one.append(out)
        log_one.append(logs)
        rows = before(out[0], pair_one[-1]) if s else out[0]
        parts, done = pair_start(mm_back(rows, output_self))
        pair_one.append(parts)

    encoder_all = ctx_gather(encoder_states, False, 1, done)
    down = first_whole(before(down_pieces, done), down_pieces[0].shape[0])
    kv_two = [low_cast(mm(before(encoder_all[s], down), pair_cross)) for s in every]
    after_one, norm_two, q_two, att_two, log_two, pair_two = [], [], [], [], [], []
    done = (done, kv_two)
    for s in every:
        after_one.append(source[s] + pair_end(pair_one[s], done))
        norm_two.append(rms_forward(after_one[s], gain_cross))
        q_two.append(low_cast(mm(norm_two[s][2], query_cross)))
        out, logs = attend_forward(
            q_two[s][None], kv_two[s][None], one(query_docs, s), one(enc_docs, s)
        )
        att_two.append(out)
        log_two.append(logs)
        rows = out[0] if s else before(out[0], pair_one[-1])
        parts, done = pair_start(mm_back(rows, output_cross))
        pair_two.append(parts)

    grad_units = [mm(before(out_cotangent[s], done), down) for s in every]
    after_two, norm_three, units_out, grads_gate, grads_up, pair_three = [], [], [], [], [], []
    done = (done, grad_units)
    for s in every:
        after_two.append(after_one[s] + pair_end(pair_two[s], done))
        norm_three.append(rms_forward(after_two[s], gain_ffn))
        both_rows = mm(norm_three[s][2], gate_up)
        up_rows = both_rows[:, units:]
        activated, gelu_pull = jax.vjp(
            lambda v: jax.nn.gelu(v, approximate=True), both_rows[:, :units]
        )
        units_out.append(low_cast(activated * up_rows))
        grads_gate.append(low_cast(gelu_pull(grad_units[s] * up_rows)[0]))
        grads_up.append(low_cast(grad_units[s] * activated))
        parts, done = pair_start(
            mm_back(grads_gate[s], gate_up[:, :units]) + mm_back(grads_up[s], gate_up[:, units:])
        )
        pair_three.append(parts)
    cotangent = [out_cotangent[s] for s in every]
    low_three = [n[2] for n in norm_three]
    ffn_blocks = gradient_blocks(
        [(low_three, grads_gate), (low_three, grads_up), (cotangent, units_out)], units
    )
    ffn_part = lax.psum_scatter(ffn_blocks, ("fsdp", "ctx"), scatter_dimension=0, tiled=True)

    res_two, low_two, dq_two, dk_two, dv_two, gain_three, pair_four = [], [], [], [], [], [], []
    done = (done, ffn_blocks)
    for s in every:
        grad_from, gain = rms_backward(
            pair_end(pair_three[s], done), norm_three[s][0], norm_three[s][1], gain_ffn
        )
        gain_three.append(gain)
        res_two.append(wide_cast(out_cotangent[s]) + grad_from)
        low_two.append(low_cast(res_two[s]))
        grad_attended = low_cast(mm(low_two[s], output_cross))
        dq, dk, dv = attend_backward(
            q_two[s][None], kv_two[s][None], one(query_docs, s), one(enc_docs, s),
            att_two[s], log_two[s], grad_attended[None],
        )
        dq_two.append(dq[0])
        dk_two.append(dk[0])
        dv_two.append(dv[0])
        rows = before(dq[0], pair_four[-1]) if s else dq[0]
        parts, done = pair_start(mm_back(rows, query_cross))
        pair_four.append(parts)
    encoder_rows = [encoder_all[s] for s in every]
    middle, middle_blocks = fold_start(
        [
            (before([n[2] for n in norm_two], done), dq_two),
            (encoder_rows, dk_two),
            (encoder_rows, dv_two),
            (low_two, [a[0] for a in att_two]),
        ],
        hw,
    )

    res_one, low_one, dq_one, dk_one, dv_one, gain_two, line_grads, folds = (
        [], [], [], [], [], [], [], [],
    )
    encoder_fold, encoder_done = block_fold_start(before(dk_two, middle_blocks), dv_two)
    done = (done, middle_blocks, encoder_done)
    pair_states, pair_out, pair_six = None, None, []
    for s in every:
        grad_from, gain = rms_backward(
            pair_end(pair_four[s], done), norm_two[s][0], norm_two[s][1], gain_cross
        )
        gain_two.append(gain)
        res_one.append(res_two[s] + grad_from)
        low_one.append(low_cast(res_one[s]))
        grad_attended = low_cast(mm(low_one[s], output_self))
        if s == 0:
            middle, done = fold_fsdp_first(middle, grad_attended)
            encoder_fold, encoder_done = block_fold_high(encoder_fold, False, done)
            done = (done, encoder_done)
        else:
            folds[s - 1], done = block_fold_high(folds[s - 1], True, grad_attended)
            if s == 1:
                rows = jnp.concatenate(before(units_out, done), axis=0)
                pair_out, own = pair_start(mm_back(rows, down))
                done = (done, own)
        dq, dk, dv, line = attend_backward(
            q_one[s][None], kv_one[s][None], one(query_docs, s), one(dec_docs, s),
            att_one[s], log_one[s], before(grad_attended, done)[None], place, lines,
        )
        dq_one.append(dq[0])
        dk_one.append(dk[0])
        dv_one.append(dv[0])
        line_grads.append(line)
        if s == 0:
            folded = block_fold_end(encoder_fold, dk)
            pair_states, own = pair_start(mm_back(folded, pair_cross))
            fold, done = block_fold_start(before([dk[0]], own), [dv[0]])
            folds.append(fold)
        elif s < seqs - 1:
            fold, done = block_fold_start([dk[0]], [dv[0]])
            folds.append(fold)

    last = seqs - 1
    for s in range(last):
        folded = block_fold_end(folds[s], dk_one[last])
        parts, done = pair_start(mm_back(dq_one[s], query_self) + mm_back(folded, pair_self))
        pair_six.append(parts)
    first, done = fold_start(
        [(before(low_one, done), [a[0] for a in att_one]), ([n[2] for n in norm_one], dq_one)], hw
    )
    fold, done = block_fold_start(before([dk_one[last]], done), [dv_one[last]])
    states = pair_end(pair_states, done)
    grad_states = low_cast(states).reshape(seqs, -1, width)
    first, done = fold_fsdp_first(first, (done, grad_states))
    fold, done = block_fold_high(fold, True, done)
    second, second_blocks = fold_start([(before(norm_all, done), dk_one), (norm_all, dv_one)], hw)
    folded = block_fold_end(fold, second_blocks)
    parts, done = pair_start(mm_back(dq_one[last], query_self) + mm_back(folded, pair_self))
    pair_six.append(parts)
    second, done = fold_high(second, done)
    middle, done = fold_high_last(middle, done)
    out_rows = pair_end(pair_out, done)
    layer_output = [
        low_cast(after_two[s] + out_rows[s * row_count : (s + 1) * row_count]) for s in every
    ]
    first, done = fold_high_last(first, layer_output)
    grad_input, gain_one = [], []
    for s in every:
        grad_from, gain = rms_backward(
            pair_end(pair_six[s], done), norm_one[s][0], norm_one[s][1], gain_self
        )
        gain_one.append(gain)
        grad_input.append(low_cast(res_one[s] + grad_from))
    line_total = sum(line_grads)[:, :2].reshape(head_count, row_count + length)
    spread = lax.dynamic_update_slice_in_dim(
        jnp.zeros((head_count, 2 * length), jnp.float32), line_total, offset, 1
    )[:, length:]
    grad_bias = jnp.dot(spread, bucket_onehot, precision=lax.Precision.HIGHEST).T
    totals = [sum(g).reshape(shards, gain_rows) for g in (gain_one, gain_two, gain_three)]
    totals = jnp.concatenate(totals + [grad_bias.reshape(shards, -1)], axis=1)
    second, done = fold_fsdp(second, totals, grad_input)
    middle_part = fold_own(middle, done)
    outer = spread_high(jnp.concatenate([before(ffn_part, done), middle_part], axis=1))
    first_part_sum = fold_own(first, outer[0])
    second_part = fold_own(second, first_part_sum)
    inner = jnp.concatenate(
        [jnp.pad(first_part_sum, ((0, EXTRA), (0, 0))),
         second_part],
        axis=1,
    )
    outer, done = spread_low(outer, inner)
    inner = spread_high(inner)
    edge = 3 * units
    ffn_gate_grad, ffn_up_grad, ffn_down_grad, cross_q, cross_k, cross_v, cross_o = spread_end(
        outer,
        [
            (0, units, False), (units, 2 * units, False), (2 * units, edge, True),
            (edge, edge + hw, False), (edge + hw, edge + 2 * hw, False),
            (edge + 2 * hw, edge + 3 * hw, False), (edge + 3 * hw, edge + 4 * hw, True),
        ],
    )
    inner, done = spread_low(inner, ffn_gate_grad)
    self_o, self_q, self_k, self_v, sums = spread_end(
        inner,
        [(0, hw, True), (hw, 2 * hw, False), (2 * hw, 3 * hw, False), (3 * hw, 4 * hw, False)],
        EXTRA,
    )
    sums = sums[0, 2 * hw :]
    gain_grads = [sums[gain_rows * i : gain_rows * (i + 1)] for i in range(3)]
    bias_grad = sums[3 * gain_rows : 3 * gain_rows + bucket_rows * head_count]
    return (
        jnp.stack(layer_output),
        jnp.stack(grad_input),
        grad_states,
        gain_grads[0],
        self_q,
        self_k,
        self_v,
        self_o,
        bias_grad.reshape(bucket_rows, head_count),
        gain_grads[1],
        cross_q,
        cross_k,
        cross_v,
        cross_o,
        gain_grads[2],
        ffn_gate_grad,
        ffn_up_grad,
        ffn_down_grad,
    )


def solution(mesh):
    in_specs = (
        P("fsdp", "ctx", None),
        P("fsdp", "ctx", None),
        P("fsdp", None),
        P("fsdp", None),
        P(),
        P("fsdp", "ctx", None),
        P("fsdp"),
        P("fsdp", "tp"),
        P("fsdp", "tp"),
        P("fsdp", "tp"),
        P("tp", "fsdp"),
        P("fsdp", "tp"),
        P("fsdp"),
        P("fsdp", "tp"),
        P("fsdp", "tp"),
        P("fsdp", "tp"),
        P("tp", "fsdp"),
        P("fsdp"),
        P("fsdp", "tp"),
        P("fsdp", "tp"),
        P("tp", "fsdp"),
    )
    out_specs = (
        P("fsdp", "ctx", None),
        P("fsdp", "ctx", None),
        P("fsdp", "ctx", None),
        P("fsdp"),
        P("fsdp", "tp"),
        P("fsdp", "tp"),
        P("fsdp", "tp"),
        P("tp", "fsdp"),
        P("fsdp", "tp"),
        P("fsdp"),
        P("fsdp", "tp"),
        P("fsdp", "tp"),
        P("fsdp", "tp"),
        P("tp", "fsdp"),
        P("fsdp"),
        P("fsdp", "tp"),
        P("fsdp", "tp"),
        P("tp", "fsdp"),
    )
    return jax.shard_map(body, mesh=mesh, in_specs=in_specs, out_specs=out_specs, check_vma=False)
```

```python
import functools
import jax
import jax.numpy as jnp
from jax import lax
from jax.experimental import pallas as pl
from jax.experimental.pallas import tpu as pltpu
from jax.sharding import PartitionSpec as P

EPSILON = 1e-06
NEGATIVE = -1e30
EXTRA = 16
TINY = pl.CostEstimate(flops=1, bytes_accessed=1, transcendentals=0)
LANES = 128
STRIP = 64
CHUNK = 256
NT = (((1,), (1,)), ((), ()))
NN = (((1,), (0,)), ((), ()))


def dot(lhs, rhs, dims=NN):
    return lax.dot_general(lhs, rhs, dims, preferred_element_type=jnp.float32)


def fill_mask(mask_ref, seg_row, seg_col_ref, offset_ref, causal):
    rows = seg_row.shape[1]
    keys = mask_ref.shape[0]
    for start in range(0, keys, CHUNK):
        size = min(CHUNK, keys - start)
        seen = seg_col_ref[0, pl.ds(start, size), :] == seg_row
        if causal:
            key_place = lax.broadcasted_iota(jnp.int32, (size, rows), 0) + start
            query_place = lax.broadcasted_iota(jnp.int32, (size, rows), 1) + offset_ref[0, 0]
            seen = seen & (key_place <= query_place)
        mask_ref[pl.ds(start, size), :] = jnp.where(seen, 0.0, NEGATIVE)


def fill_bias(bias_ref, head, line):
    width = line.shape[1]
    base = jnp.broadcast_to(line, (8, width))
    row = lax.broadcasted_iota(jnp.int32, (8, width), 0)
    for bit in (1, 2, 4):
        base = jnp.where((row & bit) != 0, pltpu.roll(base, bit, 1), base)
    for block in range(LANES // 8):
        bias_ref[head, pl.ds(8 * block, 8), :] = pltpu.roll(base, 8 * block, 1) if block else base


def fold_diagonals(total):
    width = total.shape[1]
    half = total.shape[0] // 2
    while half >= 8:
        total = total[:half] + pltpu.roll(total[half:], width - half, 1)
        half //= 2
    row = lax.broadcasted_iota(jnp.int32, (8, width), 0)
    for bit in (4, 2, 1):
        total = jnp.where((row & bit) != 0, pltpu.roll(total, width - bit, 1), total)
    return jnp.sum(total, axis=0, keepdims=True)


def head_mask(rows, head):
    lane = lax.broadcasted_iota(jnp.int32, (rows, LANES), 1)
    return (lane // (LANES // 2)) == head


def add_bias(scores, bias_ref, head, start, keys, rows):
    parts = []
    for sub in range(0, scores.shape[0], LANES):
        at = keys - (start + sub)
        parts.append(scores[sub : sub + LANES] + bias_ref[head, :, at : at + rows])
    return jnp.concatenate(parts, axis=0)


def forward_kernel(causal, *refs):
    if causal:
        (offset_ref, line_ref, seg_row_ref, seg_col_ref, q_ref, k_ref, v_ref, out_ref, log_ref,
         mask_ref, score_ref, bias_ref) = refs
    else:
        (seg_row_ref, seg_col_ref, q_ref, k_ref, v_ref, out_ref, log_ref,
         mask_ref, score_ref) = refs
        offset_ref = None
    pair = pl.program_id(0)
    seq = pl.program_id(1)
    rows = q_ref.shape[1]
    keys = k_ref.shape[1]

    @pl.when(pair == 0)
    def _():
        fill_mask(mask_ref.at[seq], seg_row_ref[0], seg_col_ref, offset_ref, causal)

    if causal:

        @pl.when(seq == 0)
        def _():
            for head in range(2):
                fill_bias(bias_ref, head, line_ref[0, pl.ds(head, 1), :])

    q = q_ref[0]
    v_turned = v_ref[0].T
    half = LANES // 2
    outs = []
    logs = []
    for head in range(2):
        q_head = jnp.where(head_mask(rows, head), q, jnp.zeros_like(q))
        highest = None
        for start in range(0, keys, CHUNK):
            scores = dot(k_ref[0, pl.ds(start, CHUNK), :], q_head, NT)
            scores = scores + mask_ref[seq, pl.ds(start, CHUNK), :]
            if causal:
                scores = add_bias(scores, bias_ref, head, start, keys, rows)
            score_ref[pl.ds(start, CHUNK), :] = scores
            top = jnp.max(scores, axis=0, keepdims=True)
            highest = top if highest is None else jnp.maximum(highest, top)
        total = None
        attended = None
        for start in range(0, keys, CHUNK):
            grown = jnp.exp(score_ref[pl.ds(start, CHUNK), :] - highest)
            part = jnp.sum(grown, axis=0, keepdims=True)
            piece = dot(v_turned[half * head : half * head + half, start : start + CHUNK],
                        grown.astype(jnp.bfloat16))
            total = part if total is None else total + part
            attended = piece if attended is None else attended + piece
        outs.append(attended / total)
        logs.append(highest + jnp.log(total))
    out_ref[0] = jnp.concatenate(outs, axis=0).T.astype(jnp.bfloat16)
    log_ref[0, 0] = jnp.concatenate(logs + [jnp.zeros((6, rows), jnp.float32)], axis=0)


def backward_kernel(causal, *refs):
    if causal:
        (offset_ref, line_ref, seg_row_ref, seg_col_ref, q_ref, k_ref, v_ref, out_ref, log_ref,
         grad_ref, dq_ref, dk_ref, dv_ref, line_grad_ref, mask_ref, bias_ref, total_ref) = refs
    else:
        (seg_row_ref, seg_col_ref, q_ref, k_ref, v_ref, out_ref, log_ref,
         grad_ref, dq_ref, dk_ref, dv_ref, mask_ref) = refs
        offset_ref = None
    pair = pl.program_id(0)
    seq = pl.program_id(1)
    rows = q_ref.shape[1]
    keys = k_ref.shape[1]
    half = LANES // 2

    @pl.when(pair == 0)
    def _():
        fill_mask(mask_ref.at[seq], seg_row_ref[0], seg_col_ref, offset_ref, causal)

    if causal:

        @pl.when(seq == 0)
        def _():
            for head in range(2):
                fill_bias(bias_ref, head, line_ref[0, pl.ds(head, 1), :])
            total_ref[...] = jnp.zeros_like(total_ref)

    q = q_ref[0]
    grad = grad_ref[0]
    product = grad.astype(jnp.float32) * out_ref[0].astype(jnp.float32)
    chooser = (
        lax.broadcasted_iota(jnp.int32, (8, LANES), 1) // half
        == lax.broadcasted_iota(jnp.int32, (8, LANES), 0)
    ).astype(jnp.float32)
    inner = lax.dot_general(chooser, product, NT, precision=lax.Precision.HIGHEST,
                            preferred_element_type=jnp.float32)
    q_heads = [jnp.where(head_mask(rows, h), q, jnp.zeros_like(q)) for h in range(2)]
    grad_heads = [jnp.where(head_mask(rows, h), grad, jnp.zeros_like(grad)) for h in range(2)]
    dq = [None, None]
    for start in range(0, keys, CHUNK):
        k = k_ref[0, pl.ds(start, CHUNK), :]
        v = v_ref[0, pl.ds(start, CHUNK), :]
        k_turned = k.T
        dk = None
        dv = None
        for head in range(2):
            scores = dot(k, q_heads[head], NT)
            scores = scores + mask_ref[seq, pl.ds(start, CHUNK), :]
            if causal:
                scores = add_bias(scores, bias_ref, head, start, keys, rows)
            weights = jnp.exp(scores - log_ref[0, 0, pl.ds(head, 1), :])
            dv_part = dot(weights.astype(jnp.bfloat16), grad_heads[head])
            dw = dot(v, grad_heads[head], NT)
            ds = weights * (dw - inner[head : head + 1])
            ds_low = ds.astype(jnp.bfloat16)
            dk_part = dot(ds_low, q_heads[head])
            dq_part = dot(k_turned[half * head : half * head + half], ds_low)
            dv = dv_part if dv is None else dv + dv_part
            dk = dk_part if dk is None else dk + dk_part
            dq[head] = dq_part if dq[head] is None else dq[head] + dq_part
            if causal:
                for sub in range(0, CHUNK, LANES):
                    at = keys - (start + sub)
                    total_ref[head, :, at : at + rows] += ds[sub : sub + LANES]
        dk_ref[0, pl.ds(start, CHUNK), :] = dk.astype(jnp.bfloat16)
        dv_ref[0, pl.ds(start, CHUNK), :] = dv.astype(jnp.bfloat16)
    dq_ref[0] = jnp.concatenate(dq, axis=0).T.astype(jnp.bfloat16)
    if causal:

        @pl.when(seq == pl.num_programs(1) - 1)
        def _():
            lines = [fold_diagonals(total_ref[head]) for head in range(2)]
            lines.append(jnp.zeros((6, lines[0].shape[1]), jnp.float32))
            line_grad_ref[0] = jnp.concatenate(lines, axis=0)


def specs_for(rows, keys, pairs, causal):
    def wide(count, shift=0):
        return pl.BlockSpec((1, count, LANES), lambda p, s: (s, 0, p + shift))

    lead = []
    if causal:
        lead = [
            pl.BlockSpec((1, 1), lambda p, s: (0, 0), memory_space=pltpu.SMEM),
            pl.BlockSpec((1, 8, rows + keys), lambda p, s: (p, 0, 0)),
        ]
    lead += [
        pl.BlockSpec((1, 1, rows), lambda p, s: (s, 0, 0)),
        pl.BlockSpec((1, keys, 1), lambda p, s: (s, 0, 0)),
        wide(rows),
        wide(keys),
        wide(keys, pairs),
    ]
    return lead, wide, pl.BlockSpec((1, 1, 8, rows), lambda p, s: (s, p, 0, 0))


def attend_forward(q, kv, seg_row, seg_col, offset=None, lines=None):
    seqs, rows, width = q.shape
    keys = kv.shape[1]
    pairs = width // LANES
    causal = lines is not None
    lead, wide, logs = specs_for(rows, keys, pairs, causal)
    scratch = [pltpu.VMEM((seqs, keys, rows), jnp.float32), pltpu.VMEM((keys, rows), jnp.float32)]
    args = [seg_row, seg_col, q, kv, kv]
    if causal:
        args = [offset, lines] + args
        scratch.append(pltpu.VMEM((2, LANES, rows + keys), jnp.float32))
    return pl.pallas_call(
        functools.partial(forward_kernel, causal),
        grid=(pairs, seqs),
        in_specs=lead,
        out_specs=[wide(rows), logs],
        out_shape=[
            jax.ShapeDtypeStruct((seqs, rows, width), jnp.bfloat16),
            jax.ShapeDtypeStruct((seqs, pairs, 8, rows), jnp.float32),
        ],
        scratch_shapes=scratch,
        compiler_params=pltpu.CompilerParams(vmem_limit_bytes=16 * 1024 * 1024),
        cost_estimate=TINY,
        name="attend_forward",
    )(*args)


def attend_backward(q, kv, seg_row, seg_col, out, logs_value, grad, offset=None, lines=None):
    seqs, rows, width = q.shape
    keys = kv.shape[1]
    pairs = width // LANES
    causal = lines is not None
    lead, wide, logs = specs_for(rows, keys, pairs, causal)
    scratch = [pltpu.VMEM((seqs, keys, rows), jnp.float32)]
    args = [seg_row, seg_col, q, kv, kv, out, logs_value, grad]
    out_shape = [
        jax.ShapeDtypeStruct((seqs, rows, width), jnp.bfloat16),
        jax.ShapeDtypeStruct((seqs, keys, width), jnp.bfloat16),
        jax.ShapeDtypeStruct((seqs, keys, width), jnp.bfloat16),
    ]
    out_specs = [wide(rows), wide(keys), wide(keys)]
    if causal:
        args = [offset, lines] + args
        scratch.append(pltpu.VMEM((2, LANES, rows + keys), jnp.float32))
        scratch.append(pltpu.VMEM((2, LANES, rows + keys), jnp.float32))
        out_shape.append(jax.ShapeDtypeStruct((pairs, 8, rows + keys), jnp.float32))
        out_specs.append(pl.BlockSpec((1, 8, rows + keys), lambda p, s: (p, 0, 0)))
    return pl.pallas_call(
        functools.partial(backward_kernel, causal),
        grid=(pairs, seqs),
        in_specs=lead + [wide(rows), logs, wide(rows)],
        out_specs=out_specs,
        out_shape=out_shape,
        scratch_shapes=scratch,
        compiler_params=pltpu.CompilerParams(vmem_limit_bytes=18 * 1024 * 1024),
        cost_estimate=TINY,
        name="attend_backward",
    )(*args)


def gradient_kernel(spans, tokens, split, *refs):
    if split:
        place_ref, refs = refs[0], refs[1:]
    lhs_count = len(tokens)
    lhs_refs = refs[:lhs_count]
    seqs = (len(refs) - lhs_count - (3 if split else 2)) // len(spans)
    rhs_refs = refs[lhs_count : lhs_count + seqs * len(spans)]
    outs = refs[lhs_count + seqs * len(spans) : -1]
    turned_ref = refs[-1]
    step = pl.program_id(0)
    for index, (first, last, group) in enumerate(spans):

        @pl.when(step == first)
        def _():
            if index == 0 or spans[index - 1][2] != group:
                for s in range(seqs):
                    lhs = lhs_refs[group * seqs + s]
                    size = lhs.shape[0]
                    turned_ref[:, s * size : (s + 1) * size] = lhs[...].T

        @pl.when((step >= first) & (step < last))
        def _():
            total = None
            for s in range(seqs):
                size = lhs_refs[group * seqs + s].shape[0]
                part = dot(turned_ref[:, s * size : (s + 1) * size], rhs_refs[index * seqs + s][...])
                total = part if total is None else total + part
            if split:
                low = place_ref[0, 0]
                rows = split
                for block in range(total.shape[0] // (2 * rows)):
                    even = total[2 * block * rows : (2 * block + 1) * rows]
                    odd = total[(2 * block + 1) * rows : (2 * block + 2) * rows]
                    at = pl.ds(block * rows, rows)
                    outs[0][at, :] = jnp.where(low == 0, odd, even).astype(jnp.bfloat16)
                    outs[1][at, :] = jnp.where(low == 0, even, odd).astype(jnp.bfloat16)
            else:
                outs[0][...] = total.astype(jnp.bfloat16)


def gradient_blocks(segments, columns, place=None, split=0):
    width = segments[0][0][0].shape[1]
    lhs_args, lhs_keys, rhs_args, rhs_specs, spans, specs = [], [], [], [], [], []
    first = 0
    flops = 0
    for lhs, rhs in segments:
        count = rhs[0].shape[1] // columns
        key = tuple(id(v) for v in lhs)
        if key not in lhs_keys:
            lhs_keys.append(key)
            lhs_args.extend(lhs)
        spans.append((first, first + count, lhs_keys.index(key)))
        for value in rhs:
            flops += 2 * value.shape[0] * value.shape[1] * width

            def where(i, first=first, count=count):
                return (0, jnp.clip(i - first, 0, count - 1))

            rhs_args.append(value)
            rhs_specs.append(pl.BlockSpec((value.shape[0], columns), where))
        first += count
    for value in lhs_args:
        specs.append(pl.BlockSpec(value.shape, lambda i: (0, 0)))
    tokens = [v.shape[0] for v in lhs_args]
    longest = max(sum(v.shape[0] for v in lhs) for lhs, rhs in segments)
    out_width = first * columns
    args = lhs_args + rhs_args
    specs = specs + rhs_specs
    if split:
        args = [place] + args
        specs = [pl.BlockSpec((1, 1), lambda i: (0, 0), memory_space=pltpu.SMEM)] + specs
        shapes = [jax.ShapeDtypeStruct((width // 2, out_width), jnp.bfloat16)] * 2
        out_specs = [pl.BlockSpec((width // 2, columns), lambda i: (0, i))] * 2
    else:
        shapes = jax.ShapeDtypeStruct((width, out_width), jnp.bfloat16)
        out_specs = pl.BlockSpec((width, columns), lambda i: (0, i))
    return pl.pallas_call(
        functools.partial(gradient_kernel, spans, tokens, split),
        grid=(first,),
        in_specs=specs,
        out_specs=out_specs,
        out_shape=shapes,
        scratch_shapes=[pltpu.VMEM((width, longest), jnp.bfloat16)],
        compiler_params=pltpu.CompilerParams(vmem_limit_bytes=36 * 1024 * 1024),
        cost_estimate=TINY,
        name="weight_gradients",
    )(*args)


def mm(lhs, rhs):
    return dot(lhs, rhs)


def mm_back(lhs, rhs):
    return dot(lhs, rhs, NT)


def rms_forward(values, gain_row):
    inverse_rms = lax.rsqrt(jnp.mean(values * values, axis=-1, keepdims=True) + EPSILON)
    unit_rows = values * inverse_rms
    return unit_rows, inverse_rms, (unit_rows * gain_row).astype(jnp.bfloat16)


def rms_backward(grad_normed, unit_rows, inverse_rms, gain_row):
    grad_unit = grad_normed * gain_row
    grad_gain = jnp.sum(grad_normed * unit_rows, axis=0)
    inner_sum = jnp.mean(grad_unit * unit_rows, axis=-1, keepdims=True)
    return inverse_rms * (grad_unit - unit_rows * inner_sum), grad_gain


def low_cast(value):
    return value.astype(jnp.bfloat16)


def wide_cast(value):
    return value.astype(jnp.float32)


def ctx_shape():
    count = lax.axis_size("ctx")
    low = 2 if count % 2 == 0 else 1
    return count // low, low


def ctx_place():
    high, low = ctx_shape()
    index = lax.axis_index("ctx")
    return index // low, index % low


def swap_low(value):
    high, low = ctx_shape()
    return lax.ppermute(value, "ctx", [(i, i ^ 1) for i in range(high * low)])


def shift_high(value, step, wrap):
    high, low = ctx_shape()
    pairs = []
    for i in range(high * low):
        target = i // low + step
        if wrap or 0 <= target < high:
            pairs.append((i, (target % high) * low + i % low))
    return lax.ppermute(value, "ctx", pairs)


def shift_fsdp(value, step):
    count = lax.axis_size("fsdp")
    return lax.ppermute(value, "fsdp", [(i, (i + step) % count) for i in range(count)])


def put(buffer, value, at, axis):
    return lax.dynamic_update_slice_in_dim(buffer, jnp.expand_dims(value, axis), at, axis)


def ctx_gather(value, causal, axis, earlier):
    high, low = ctx_shape()
    at_high, at_low = ctx_place()
    pieces = [value] + [shift_high(value, step, not causal) for step in range(1, high)]
    pieces = before(pieces, earlier)
    places = [((at_high - step) % high, at_low) for step in range(high)]
    if low == 2:
        pieces = pieces + [swap_low(piece) for piece in pieces]
        places = places + [((at_high - step) % high, 1 - at_low) for step in range(high)]
    shape = value.shape[:axis] + (high, low) + value.shape[axis:]
    held = assemble(pieces, places, shape, axis)
    shape = value.shape[:axis] + (high * low * value.shape[axis],) + value.shape[axis + 1 :]
    return held.reshape(shape)


def gather_rows(shards, earlier):
    count = lax.axis_size("ctx")
    rows = shards[0].shape[0] // count
    start = lax.axis_index("ctx") * rows
    shards = before(shards, earlier)
    parts = [lax.dynamic_slice_in_dim(s, start, rows, 0) for s in shards]
    part = jnp.concatenate(parts, axis=1) if len(parts) > 1 else parts[0]
    return lax.all_gather(part, ("fsdp", "ctx"), axis=0, tiled=True)


def before(value, *earlier):
    return lax.optimization_barrier((value, earlier))[0]


def assemble_kernel(lead, place_ref, *refs):
    pieces, out_ref = refs[:-1], refs[-1]
    step = pl.program_id(0)
    for index, piece in enumerate(pieces):

        @pl.when(step == index)
        def _():
            rows = out_ref.shape[-2]
            out_ref[...] = piece[..., :rows, :].reshape(out_ref.shape)


def assemble(pieces, places, shape, lead):
    places = jnp.stack([jnp.stack([jnp.asarray(v, jnp.int32) for v in p]) for p in places])
    block = shape[:lead] + (1, 1) + shape[lead + 2 :]
    rank = len(pieces[0].shape)

    def where(i, place):
        return (0,) * lead + (place[i, 0], place[i, 1]) + (0,) * (len(shape) - lead - 2)

    return pl.pallas_call(
        functools.partial(assemble_kernel, lead),
        grid_spec=pltpu.PrefetchScalarGridSpec(
            num_scalar_prefetch=1,
            grid=(len(pieces),),
            in_specs=[pl.BlockSpec(p.shape, lambda i, place: (0,) * rank) for p in pieces],
            out_specs=pl.BlockSpec(block, where),
        ),
        out_shape=jax.ShapeDtypeStruct(shape, pieces[0].dtype),
        compiler_params=pltpu.CompilerParams(vmem_limit_bytes=16 * 1024 * 1024),
        cost_estimate=TINY,
        name="assemble",
    )(places, *pieces)


def first_part(shards):
    high, low = ctx_shape()
    at_high, at_low = ctx_place()
    rows = shards[0].shape[0] // low
    parts = [lax.dynamic_slice_in_dim(s, at_low * rows, rows, 0) for s in shards]
    return jnp.concatenate(parts, axis=1) if len(parts) > 1 else parts[0]


def first_pieces(part):
    count = lax.axis_size("fsdp")
    if count > 8:
        held = lax.all_gather(part, "fsdp", axis=0, tiled=False)
        index = lax.axis_index("fsdp")
        return [
            lax.dynamic_index_in_dim(held, (index - step) % count, 0, False)
            for step in range(count)
        ]
    return [part] + [shift_fsdp(part, step) for step in range(1, count)]


def first_whole(pieces, rows):
    count = lax.axis_size("fsdp")
    index = lax.axis_index("fsdp")
    high, low = ctx_shape()
    at_high, at_low = ctx_place()
    columns = pieces[0].shape[1]
    places = [((index - step) % count, at_low) for step in range(count)]
    if low == 2:
        pieces = pieces + [swap_low(piece) for piece in pieces]
        places = places + [((index - step) % count, 1 - at_low) for step in range(count)]
    whole = assemble(pieces, places, (count, low, rows, columns), 0)
    return whole.reshape(count * low * rows, columns)


def gather_small(value):
    count = lax.axis_size("fsdp")
    index = lax.axis_index("fsdp")
    if count > 8:
        return lax.all_gather(value, "fsdp", axis=0, tiled=False)
    held = put(jnp.zeros((count,) + value.shape, value.dtype), value, index, 0)
    for step in range(1, count):
        held = put(held, shift_fsdp(value, step), (index - step) % count, 0)
    return held


def fold_start(segments, columns, arrive=None):
    high, low = ctx_shape()
    at_high, at_low = ctx_place()
    count = lax.axis_size("fsdp")
    width = segments[0][0][0].shape[1]
    rows = width // (count * high * low)
    shape = (count, high, rows, -1)
    if low == 2:
        place = jnp.full((1, 1), at_low, jnp.int32)
        away, kept = gradient_blocks(segments, columns, place, rows)
        done = away
        if arrive is not None:
            arrive, away = before((arrive, away), away)
            done = (arrive, done)
        return [kept.reshape(shape), swap_low(away).reshape(shape)], done
    kept = gradient_blocks(segments, columns)
    return [kept.reshape(shape)], kept if arrive is None else (before(arrive, kept), kept)


def fold_high(parts, earlier=()):
    high, low = ctx_shape()
    at_high, at_low = ctx_place()
    parts = before(parts, earlier)
    found, sent = [], []
    for step in range(1, high):
        mine, piece = split_sum(parts, [at_high, (at_high + step) % high])
        found = found or [mine]
        sent.append(piece)
        found.append(shift_high(piece, step, True))
    return found, (found[0], sent)


def fold_fsdp(parts, lines, earlier=()):
    count = lax.axis_size("fsdp")
    index = lax.axis_index("fsdp")
    parts, lines = before((parts, lines), earlier)
    small = jnp.zeros((count, EXTRA, parts[0].shape[2]), jnp.bfloat16)
    small = small.at[:, 0, : lines.shape[1]].set(low_cast(lines))
    if count > 8:
        whole = low_cast(sum(wide_cast(p) for p in parts))
        whole = jnp.concatenate([whole, small], axis=1)
        flat = whole.reshape((-1,) + whole.shape[2:])
        return [lax.psum_scatter(flat, "fsdp", scatter_dimension=0, tiled=True)], whole

    def part(at):
        total = sum(wide_cast(lax.dynamic_index_in_dim(p, at, 0, False)) for p in parts)
        line = lax.dynamic_index_in_dim(small, at, 0, False)
        return jnp.concatenate([low_cast(total), line], axis=0)

    sent = [part((index + step) % count) for step in range(1, count)]
    mine = part(index)
    moved = [shift_fsdp(piece, step + 1) for step, piece in enumerate(sent)]
    return [mine] + moved, (mine, sent)


def fold_fsdp_first(halves, earlier=()):
    count = lax.axis_size("fsdp")
    index = lax.axis_index("fsdp")
    halves = before(halves, earlier)
    if count > 8:
        whole = low_cast(sum(wide_cast(h) for h in halves))
        flat = whole.reshape((-1,) + whole.shape[2:])
        part = lax.psum_scatter(flat, "fsdp", scatter_dimension=0, tiled=True)
        return [part.reshape(whole.shape[1:])], whole

    def part(at):
        return low_cast(sum(wide_cast(lax.dynamic_index_in_dim(h, at, 0, False)) for h in halves))

    sent = [part((index + step) % count) for step in range(1, count)]
    mine = part(index)
    moved = [shift_fsdp(piece, step + 1) for step, piece in enumerate(sent)]
    return [mine] + moved, (mine, sent)


def fold_high_last(parts, earlier=()):
    high, low = ctx_shape()
    at_high, at_low = ctx_place()
    parts = before(parts, earlier)

    def part(at):
        return low_cast(sum(wide_cast(lax.dynamic_index_in_dim(p, at, 0, False)) for p in parts))

    sent = [part((at_high + step) % high) for step in range(1, high)]
    mine = part(at_high)
    moved = [shift_high(piece, step + 1, True) for step, piece in enumerate(sent)]
    return [mine] + moved, (mine, sent)


def swap_fsdp(value, bit):
    count = lax.axis_size("fsdp")
    return lax.ppermute(value, "fsdp", [(i, i ^ bit) for i in range(count)])


def doubles(count):
    return count <= 8 and count & (count - 1) == 0


def fold_fsdp_start(parts, lines=None, earlier=()):
    count = lax.axis_size("fsdp")
    index = lax.axis_index("fsdp")
    parts, lines = before((parts, lines), earlier)
    rest = parts[0].shape[1:]
    small = None
    if lines is not None:
        small = jnp.zeros((count, EXTRA, rest[-1]), jnp.bfloat16)
        small = small.at[:, 0, : lines.shape[1]].set(low_cast(lines))
    if not doubles(count):
        whole = low_cast(sum(wide_cast(p) for p in parts))
        if small is not None:
            whole = jnp.concatenate([whole, small], axis=1)
        flat = whole.reshape((-1,) + whole.shape[2:])
        part = lax.psum_scatter(flat, "fsdp", scatter_dimension=0, tiled=True)
        return [part.reshape((1,) + whole.shape[1:])], whole
    views = [p.reshape((count // 2, 2) + (-1, rest[-1])) for p in parts]
    if small is not None:
        small = small.reshape(count // 2, 2, EXTRA, rest[-1])
    mine, sent = split_sum(views, [index % 2, 1 - index % 2], small)
    shape = (count // 2,) + (rest if small is None else mine.shape[1:])
    return [mine.reshape(shape), swap_fsdp(sent, 1).reshape(shape)], (mine, sent)


def fold_fsdp_rest(parts, earlier=()):
    count = lax.axis_size("fsdp")
    index = lax.axis_index("fsdp")
    parts = before(parts, earlier)
    done = parts[0]
    bit = 2
    while doubles(count) and bit < count:
        rest = parts[0].shape[1:]
        views = [p.reshape((p.shape[0] // 2, 2) + (-1, rest[-1])) for p in parts]
        at = (index // bit) % 2
        mine, sent = split_sum(views, [at, 1 - at])
        done = (mine, sent)
        parts = [v.reshape((-1,) + rest) for v in (mine, swap_fsdp(sent, bit))]
        bit *= 2
    return parts, done


def fold_own(parts, earlier=()):
    parts = before(parts, earlier)
    total = add_parts(parts) if len(parts) > 1 else parts[0]
    return total.reshape(-1, total.shape[-1])


def spread_high(part):
    high, low = ctx_shape()
    return [part] + [shift_high(part, step, True) for step in range(1, high)]


def spread_low(parts, earlier=()):
    high, low = ctx_shape()
    parts = before(parts, earlier)
    return parts, [swap_low(p) if low == 2 else p for p in parts]


def finish_kernel(high, low, cuts, extra, place_ref, *refs):
    mine_refs, other_refs, outs = refs[:high], refs[high : 2 * high], refs[2 * high :]
    rows = mine_refs[0].shape[0] - extra

    def chosen(at_high, at_low, start, stop):
        step = lax.rem(place_ref[0, 0] - at_high + high, high)
        value = None
        for index in range(high):
            mine = mine_refs[index][:rows, start:stop]
            other = other_refs[index][:rows, start:stop]
            piece = jnp.where(place_ref[0, 1] == at_low, mine, other)
            value = piece if value is None else jnp.where(step == index, piece, value)
        return wide_cast(value)

    for (start, stop, turned), out in zip(cuts, outs):
        blocks = [chosen(h, l, start, stop) for h in range(high) for l in range(low)]
        if turned:
            out[...] = jnp.concatenate(blocks, axis=0).T
        else:
            for index, block in enumerate(blocks):
                out[pl.ds(index * rows, rows), :] = block
    if extra:
        total = None
        for ref in mine_refs + (other_refs if low == 2 else ()):
            line = wide_cast(ref[rows:, :])
            total = line if total is None else total + line
        outs[-1][...] = total


def spread_end(pair, cuts, extra=0):
    high, low = ctx_shape()
    at_high, at_low = ctx_place()
    mine, other = pair
    rows = mine[0].shape[0] - extra
    shapes = []
    for start, stop, turned in cuts:
        shape = (high * low * rows, stop - start)
        shapes.append(jax.ShapeDtypeStruct(shape[::-1] if turned else shape, jnp.float32))
    if extra:
        shapes.append(jax.ShapeDtypeStruct((extra, mine[0].shape[1]), jnp.float32))
    place = jnp.stack([at_high, at_low]).astype(jnp.int32).reshape(1, 2)
    vmem = pl.BlockSpec(memory_space=pltpu.VMEM)
    return pl.pallas_call(
        functools.partial(finish_kernel, high, low, cuts, extra),
        in_specs=[pl.BlockSpec(memory_space=pltpu.SMEM)] + [vmem] * (2 * high),
        out_specs=[vmem] * len(shapes),
        out_shape=shapes,
        compiler_params=pltpu.CompilerParams(vmem_limit_bytes=20 * 1024 * 1024),
        cost_estimate=TINY,
        name="finish",
    )(place, *mine, *other)


def block_fold_start(lefts, rights):
    high, low = ctx_shape()
    at_high, at_low = ctx_place()
    size = lefts[0].shape[0] // (high * low)

    def part(at):
        views = [v.reshape(high, low, size, -1) for v in lefts + rights]
        views = [lax.dynamic_index_in_dim(v, at, 1, False) for v in views]
        views = [
            jnp.concatenate([views[i], views[len(lefts) + i]], axis=-1) for i in range(len(lefts))
        ]
        return jnp.concatenate(views, axis=1) if len(views) > 1 else views[0]

    if low == 1:
        whole = part(0)
        return [whole], whole
    away = part(1 - at_low)
    kept = part(at_low)
    return [kept, swap_low(away)], (kept, away)


def block_fold_high(halves, causal, earlier=()):
    high, low = ctx_shape()
    at_high, at_low = ctx_place()
    halves = before(halves, earlier)

    def part(at):
        return low_cast(sum(wide_cast(lax.dynamic_index_in_dim(h, at, 0, False)) for h in halves))

    sent = [part((at_high - step) % high) for step in range(1, high)]
    mine = part(at_high)
    moved = [shift_high(piece, -step - 1, not causal) for step, piece in enumerate(sent)]
    return [mine] + moved, (mine, sent)


def block_fold_end(parts, earlier=()):
    parts = before(parts, earlier)
    return low_cast(sum(wide_cast(p) for p in parts))


def norm_backward(parts, rest_ref, values_ref, gain_ref, out_ref, low_ref, gain_out_ref):
    gain = wide_cast(gain_ref[...])
    total = jnp.zeros((8, gain.shape[1]), jnp.float32)
    for start in range(0, rest_ref.shape[0], STRIP):
        at = pl.ds(start, STRIP)
        unit, inverse, normed = rms_rows(wide_cast(values_ref[at, :]), gain)
        grad = sum(wide_cast(p[at, :]) for p in parts)
        product = grad * unit
        for row in range(0, STRIP, 8):
            total = total + product[row : row + 8]
        inner = jnp.mean(product * gain, axis=1, keepdims=True)
        result = wide_cast(rest_ref[at, :]) + inverse * (grad * gain - unit * inner)
        if out_ref is not None:
            out_ref[at, :] = result
        low_ref[at, :] = low_cast(result)
    gain_out_ref[...] = total


def rms_rows(values, gain):
    inverse = lax.rsqrt(jnp.mean(values * values, axis=1, keepdims=True) + EPSILON)
    unit = values * inverse
    return unit, inverse, low_cast(unit * gain)


def project_end_kernel(mine_ref, moved_ref, dq_ref, wide_ref, own_ref):
    width = dq_ref.shape[1]
    folded = low_cast(wide_cast(mine_ref[...]) + wide_cast(moved_ref[...]))
    for start in range(0, own_ref.shape[1], CHUNK):
        at = pl.ds(start, CHUNK)
        total = dot(dq_ref[...], wide_ref[at, :width], NT)
        own_ref[:, at] = low_cast(total + dot(folded, wide_ref[at, width:], NT))


def project_end(parts, dq, wide_weights):
    vmem = pl.BlockSpec(memory_space=pltpu.VMEM)
    return pl.pallas_call(
        project_end_kernel,
        in_specs=[vmem] * 4,
        out_specs=vmem,
        out_shape=jax.ShapeDtypeStruct((dq.shape[0], wide_weights.shape[0]), jnp.bfloat16),
        compiler_params=pltpu.CompilerParams(vmem_limit_bytes=16 * 1024 * 1024),
        cost_estimate=TINY,
        name="project_end",
    )(parts[0], parts[1], dq, wide_weights)


def last_norm_kernel(part_ref, moved_ref, rest_ref, values_ref, gain_ref, low_ref, gain_out_ref):
    norm_backward([part_ref, moved_ref], rest_ref, values_ref, gain_ref, None, low_ref,
                  gain_out_ref)


def last_norm(parts, rest, values, gain):
    vmem = pl.BlockSpec(memory_space=pltpu.VMEM)
    return pl.pallas_call(
        last_norm_kernel,
        in_specs=[vmem] * 5,
        out_specs=[vmem] * 2,
        out_shape=[jax.ShapeDtypeStruct(rest.shape, jnp.bfloat16), jax.ShapeDtypeStruct((8, rest.shape[1]), jnp.float32)],
        compiler_params=pltpu.CompilerParams(vmem_limit_bytes=16 * 1024 * 1024),
        cost_estimate=TINY,
        name="last_norm",
    )(parts[0], parts[1], rest, values, gain)


def add_kernel(count, *refs):
    total = sum(wide_cast(r[...]) for r in refs[:count])
    refs[count][...] = low_cast(total)


def add_parts(parts):
    vmem = pl.BlockSpec(memory_space=pltpu.VMEM)
    return pl.pallas_call(
        functools.partial(add_kernel, len(parts)),
        in_specs=[vmem] * len(parts),
        out_specs=vmem,
        out_shape=jax.ShapeDtypeStruct(parts[0].shape, jnp.bfloat16),
        compiler_params=pltpu.CompilerParams(vmem_limit_bytes=16 * 1024 * 1024),
        cost_estimate=TINY,
        name="add_parts",
    )(*parts)


def split_sum(parts, places, extra=None):
    shape = parts[0].shape
    rest = (0,) * (len(shape) - 2)
    places = jnp.stack([jnp.asarray(v, jnp.int32) for v in places])
    specs = []
    for which in range(2):
        for part in parts:
            if len(part.shape) == len(shape):
                spec = pl.BlockSpec(
                    (1, 1) + shape[2:], lambda i, place, which=which: (i, place[which]) + rest
                )
            else:
                spec = pl.BlockSpec(
                    (1, 1, 1) + shape[2:],
                    lambda i, place, which=which: (i, place[which], place[2]) + rest,
                )
            specs.append(spec)
    args = list(parts) + list(parts)
    added = 0
    if extra is not None:
        added = extra.shape[2]
        args += [extra, extra]
        for which in range(2):
            specs.append(
                pl.BlockSpec(
                    (1, 1) + extra.shape[2:],
                    lambda i, place, which=which: (i, place[which]) + rest,
                )
            )
    out_shape = (shape[2] + added,) + shape[3:]
    out = jax.ShapeDtypeStruct((shape[0],) + out_shape, jnp.bfloat16)
    out_spec = pl.BlockSpec((1,) + out_shape, lambda i, place: (i,) + rest)

    def kernel(place_ref, *refs):
        for which in range(2):
            total = None
            for ref in refs[which * len(parts) : (which + 1) * len(parts)]:
                value = wide_cast(ref[...]).reshape(shape[2:])
                total = value if total is None else total + value
            out_ref = refs[len(args) + which]
            out_ref[0, : shape[2]] = low_cast(total)
            if added:
                out_ref[0, shape[2] :] = refs[2 * len(parts) + which][0, 0]

    return pl.pallas_call(
        kernel,
        grid_spec=pltpu.PrefetchScalarGridSpec(
            num_scalar_prefetch=1,
            grid=(shape[0],),
            in_specs=specs,
            out_specs=[out_spec, out_spec],
        ),
        out_shape=[out, out],
        compiler_params=pltpu.CompilerParams(vmem_limit_bytes=16 * 1024 * 1024),
        cost_estimate=TINY,
        name="split_sum",
    )(places, *args)


def pair_start(partial):
    own = low_cast(partial)
    count = lax.axis_size("tp")
    moved = [
        lax.ppermute(own, "tp", [(i, (i + step) % count) for i in range(count)])
        for step in range(1, count)
    ]
    return [own] + moved, own


def pair_end(parts, earlier=()):
    parts = before(parts, earlier)
    return sum(wide_cast(p) for p in parts)


def body(
    hidden_in,
    encoder_states,
    dec_segments,
    enc_segments,
    bucket_table,
    out_cotangent,
    self_gain,
    self_query,
    self_key,
    self_value,
    self_output,
    position_bias,
    cross_gain,
    cross_query,
    cross_key,
    cross_value,
    cross_output,
    ffn_gain,
    ffn_gate,
    ffn_up,
    ffn_down,
):
    shards = lax.axis_size("fsdp")
    seqs, row_count, width = hidden_in.shape
    length = dec_segments.shape[1]
    hw = self_query.shape[1]
    units = ffn_gate.shape[1]
    bucket_rows, head_count = position_bias.shape
    bucket_count = bucket_rows * shards
    gain_rows = self_gain.shape[0]
    offset = lax.axis_index("ctx") * row_count
    every = range(seqs)
    last = seqs - 1

    small = jnp.concatenate([self_gain, cross_gain, ffn_gain, position_bias.reshape(-1)])
    line = jnp.zeros((EXTRA, 3 * hw), jnp.bfloat16).at[0, : small.shape[0]].set(small)
    qkv_part = first_part([self_query, self_key, self_value])
    first_rows = qkv_part.shape[0]
    qkv_part = jnp.concatenate([qkv_part, line], axis=0)
    first_arrived = first_pieces(qkv_part)
    shard = lax.axis_index("fsdp")
    small = jnp.stack([piece[first_rows, : small.shape[0]] for piece in first_arrived])
    small = jnp.stack(
        [lax.dynamic_index_in_dim(small, (shard - i) % shards, 0, False) for i in range(shards)]
    )
    gain_self, gain_cross, gain_ffn = [
        wide_cast(small[:, gain_rows * i : gain_rows * (i + 1)].reshape(width)) for i in range(3)
    ]
    bias_table = wide_cast(small[:, 3 * gain_rows :].reshape(bucket_count, head_count))
    first_weights = first_whole(first_arrived, first_rows)
    hidden_all = ctx_gather(before(hidden_in, qkv_part), True, 1, first_arrived[-1])
    source = [wide_cast(hidden_in[s]) for s in every]
    norm_one = [rms_forward(source[s], gain_self) for s in every]
    norm_all = [rms_forward(wide_cast(hidden_all[s]), gain_self)[2] for s in every]
    middle_weights = gather_rows(
        [self_output.T, cross_query, cross_key, cross_value, cross_output.T], qkv_part
    )
    gate_up = gather_rows([ffn_gate, ffn_up], qkv_part)
    ffn_down, encoder_states = before((ffn_down, encoder_states), first_weights, norm_all[0])
    down_pieces = first_pieces(first_part([ffn_down.T]))
    query_self = first_weights[:, :hw]
    pair_self = first_weights[:, hw:]
    output_self = middle_weights[:, :hw]
    query_cross = middle_weights[:, hw : 2 * hw]
    pair_cross = middle_weights[:, 2 * hw : 4 * hw]
    output_cross = middle_weights[:, 4 * hw :]

    query_docs = lax.dynamic_slice_in_dim(dec_segments, offset, row_count, 1)[:, None, :]
    dec_docs = dec_segments[:, :, None]
    enc_docs = enc_segments[:, :, None]
    bucket_onehot = wide_cast(
        bucket_table[:, None] == jnp.arange(bucket_count, dtype=jnp.int32)[None, :]
    )
    distance_bias = jnp.dot(bucket_onehot, bias_table, precision=lax.Precision.HIGHEST).T
    padded = jnp.concatenate([jnp.zeros_like(distance_bias), distance_bias], axis=1)
    lines = lax.dynamic_slice_in_dim(padded, offset, row_count + length, 1)
    lines = lines.reshape(head_count // 2, 2, row_count + length)
    lines = jnp.concatenate(
        [lines, jnp.zeros((head_count // 2, 6, row_count + length), jnp.float32)], axis=1
    )
    place = jnp.full((1, 1), offset, jnp.int32)

    def one(value, s):
        return value[s : s + 1]

    q_one, kv_one, att_one, log_one, pair_one, done = [], [], [], [], [], ()
    for s in every:
        rows_all, rows_own = before((norm_all[s], norm_one[s][2]), done)
        kv_one.append(low_cast(mm(rows_all, pair_self)))
        q_one.append(low_cast(mm(rows_own, query_self)))
        out, logs = attend_forward(
            q_one[s][None], kv_one[s][None], one(query_docs, s), one(dec_docs, s), place, lines
        )
        att_one.append(out)
        log_one.append(logs)
        rows = before(out[0], pair_one[-1]) if s else out[0]
        parts, done = pair_start(mm_back(rows, output_self))
        pair_one.append(parts)

    encoder_all = ctx_gather(encoder_states, False, 1, done)
    down = first_whole(before(down_pieces, done), down_pieces[0].shape[0])
    kv_two = [low_cast(mm(before(encoder_all[s], down), pair_cross)) for s in every]
    after_one, norm_two, q_two, att_two, log_two, pair_two = [], [], [], [], [], []
    done = (done, kv_two)
    for s in every:
        after_one.append(source[s] + pair_end(pair_one[s], done))
        norm_two.append(rms_forward(after_one[s], gain_cross))
        q_two.append(low_cast(mm(norm_two[s][2], query_cross)))
        out, logs = attend_forward(
            q_two[s][None], kv_two[s][None], one(query_docs, s), one(enc_docs, s)
        )
        att_two.append(out)
        log_two.append(logs)
        rows = out[0] if s else before(out[0], pair_one[-1])
        parts, done = pair_start(mm_back(rows, output_cross))
        pair_two.append(parts)

    grad_units = [mm(before(out_cotangent[s], done), down) for s in every]
    after_two, norm_three, units_out, grads_gate, grads_up, pair_three = [], [], [], [], [], []
    done = (done, grad_units)
    for s in every:
        after_two.append(after_one[s] + pair_end(pair_two[s], done))
        norm_three.append(rms_forward(after_two[s], gain_ffn))
        both_rows = mm(norm_three[s][2], gate_up)
        up_rows = both_rows[:, units:]
        activated, gelu_pull = jax.vjp(
            lambda v: jax.nn.gelu(v, approximate=True), both_rows[:, :units]
        )
        units_out.append(low_cast(activated * up_rows))
        grads_gate.append(low_cast(gelu_pull(grad_units[s] * up_rows)[0]))
        grads_up.append(low_cast(grad_units[s] * activated))
        parts, done = pair_start(
            mm_back(grads_gate[s], gate_up[:, :units]) + mm_back(grads_up[s], gate_up[:, units:])
        )
        pair_three.append(parts)
    cotangent = [out_cotangent[s] for s in every]
    low_three = [n[2] for n in norm_three]
    ffn_blocks = gradient_blocks(
        [
            (before(low_three, done, pair_three[0]), grads_gate),
            (low_three, grads_up),
            (cotangent, units_out),
        ],
        units,
    )
    ffn_part = lax.psum_scatter(ffn_blocks, ("fsdp", "ctx"), scatter_dimension=0, tiled=True)

    res_two, low_two, dq_two, dk_two, dv_two, gain_three, pair_four = [], [], [], [], [], [], []
    done = (done, ffn_blocks)
    for s in every:
        grad_from, gain = rms_backward(
            pair_end(pair_three[s], done), norm_three[s][0], norm_three[s][1], gain_ffn
        )
        gain_three.append(gain)
        res_two.append(wide_cast(out_cotangent[s]) + grad_from)
        low_two.append(low_cast(res_two[s]))
        grad_attended = low_cast(mm(low_two[s], output_cross))
        dq, dk, dv = attend_backward(
            q_two[s][None], kv_two[s][None], one(query_docs, s), one(enc_docs, s),
            att_two[s], log_two[s], grad_attended[None],
        )
        dq_two.append(dq[0])
        dk_two.append(dk[0])
        dv_two.append(dv[0])
        rows = before(dq[0], pair_four[-1]) if s else dq[0]
        parts, done = pair_start(mm_back(rows, query_cross))
        pair_four.append(parts)
    encoder_rows = [encoder_all[s] for s in every]
    pair_out = []
    parts, done = pair_start(mm_back(before(units_out[0], done), down))
    pair_out.append(parts)
    middle, done = fold_start(
        [
            (before([n[2] for n in norm_two], done), dq_two),
            (encoder_rows, dk_two),
            (encoder_rows, dv_two),
            (low_two, [a[0] for a in att_two]),
        ],
        hw,
    )

    res_one, low_one, dq_one, dk_one, dv_one, gain_two, line_grads, folds = (
        [], [], [], [], [], [], [], [],
    )
    encoder_fold, done = block_fold_start(before(dk_two, done), dv_two)
    layer_output = []

    def finish_output(s, earlier):
        layer_output.append(low_cast(after_two[s] + pair_end(pair_out[s], earlier)))
        return layer_output[-1]

    for s in every:
        grad_from, gain = rms_backward(
            pair_end(pair_four[s], done), norm_two[s][0], norm_two[s][1], gain_cross
        )
        gain_two.append(gain)
        res_one.append(res_two[s] + grad_from)
        low_one.append(low_cast(res_one[s]))
        grad_attended = low_cast(mm(low_one[s], output_self))
        if s == 0:
            encoder_fold, done = block_fold_high(encoder_fold, False, grad_attended)
            done = finish_output(0, done)
        else:
            folds[s - 1], done = block_fold_high(folds[s - 1], True, grad_attended)
            parts, done = pair_start(mm_back(before(units_out[s], done), down))
            pair_out.append(parts)
        dq, dk, dv, line = attend_backward(
            q_one[s][None], kv_one[s][None], one(query_docs, s), one(dec_docs, s),
            att_one[s], log_one[s], before(grad_attended, done)[None], place, lines,
        )
        dq_one.append(dq[0])
        dk_one.append(dk[0])
        dv_one.append(dv[0])
        line_grads.append(line)
        if s == 0:
            folded = block_fold_end(encoder_fold, dk)
            pair_states, own = pair_start(mm_back(folded, pair_cross))
            done = own
        if s < last:
            fold, done = block_fold_start(before([dk[0]], done), [dv[0]])
            folds.append(fold)

    arrived = before((folds, pair_out[1:]), dk_one[last])
    folds, pair_out[1:] = arrived
    fold, done = block_fold_start(before([dk_one[last]], arrived), [dv_one[last]])
    pair_six = []
    for s in range(last):
        parts, done = pair_start(project_end(before(folds[s], done), dq_one[s], first_weights))
        pair_six.append(parts)
    fold, done = block_fold_high(fold, True, done)
    first, done = fold_start(
        [(before(low_one, done), [a[0] for a in att_one]), ([n[2] for n in norm_one], dq_one)], hw
    )
    second, (arrived, done) = fold_start(
        [(before(norm_all, done), dk_one), (norm_all, dv_one)], hw, (fold, pair_six)
    )
    fold, pair_six = arrived
    parts, done = pair_start(project_end(before(fold, arrived), dq_one[last], first_weights))
    pair_six.append(parts)
    ffn_spread = spread_high(before(ffn_part, done))
    middle, done = fold_fsdp_start(middle, None, ffn_spread[0])
    second, done = fold_high(second, done)
    first, done = fold_fsdp_start(first, None, done)
    grad_input, gain_one = [], []

    gain_row = gain_self.reshape(1, -1)

    def finish_sequence(s, earlier):
        rows, gain = last_norm(
            before(pair_six[s], earlier), res_one[s], hidden_in[s], gain_row
        )
        gain_one.append(jnp.sum(gain, axis=0))
        grad_input.append(rows)
        return rows

    for s in range(last):
        done = finish_sequence(s, done)
    line_grads = before(line_grads, done)
    for s in range(1, seqs):
        done = finish_output(s, done)
    ffn_spread = spread_low(ffn_spread, done)
    second = before(second, done)
    done = finish_sequence(last, second)
    line_total = sum(line_grads)[:, :2].reshape(head_count, row_count + length)
    spread = lax.dynamic_update_slice_in_dim(
        jnp.zeros((head_count, 2 * length), jnp.float32), line_total, offset, 1
    )[:, length:]
    grad_bias = jnp.dot(spread, bucket_onehot, precision=lax.Precision.HIGHEST).T
    totals = [sum(g).reshape(shards, gain_rows) for g in (gain_one, gain_two, gain_three)]
    totals = jnp.concatenate(totals + [grad_bias.reshape(shards, -1)], axis=1)
    second, done = fold_fsdp_start(second, totals, grad_input)
    middle, done = fold_fsdp_rest(middle, done)
    first, done = fold_fsdp_rest(first, done)
    second, done = fold_fsdp_rest(second, done)
    middle, done = fold_high(middle, done)
    first, done = fold_high(first, done)
    middle_sum = fold_own(middle, done)
    middle_spread = spread_high(middle_sum)
    second_sum = fold_own(second, middle_sum)
    done = second_sum
    ffn_gate_grad, ffn_up_grad, ffn_down_grad = spread_end(
        before(ffn_spread, done),
        [(0, units, False), (units, 2 * units, False), (2 * units, 3 * units, True)],
    )
    middle_spread = spread_low(middle_spread, ffn_gate_grad)
    first_sum = fold_own(first, middle_spread[0])
    inner = jnp.concatenate([jnp.pad(first_sum, ((0, EXTRA), (0, 0))), second_sum], axis=1)
    inner = spread_high(inner)
    cross_q, cross_k, cross_v, cross_o = spread_end(
        before(middle_spread, inner[0]),
        [(0, hw, False), (hw, 2 * hw, False), (2 * hw, 3 * hw, False), (3 * hw, 4 * hw, True)],
    )
    inner = spread_low(inner, cross_q)
    grad_states = low_cast(pair_end(pair_states, inner[0])).reshape(seqs, -1, width)
    self_o, self_q, self_k, self_v, sums = spread_end(
        inner,
        [(0, hw, True), (hw, 2 * hw, False), (2 * hw, 3 * hw, False), (3 * hw, 4 * hw, False)],
        EXTRA,
    )
    sums = sums[0, 2 * hw :]
    gain_grads = [sums[gain_rows * i : gain_rows * (i + 1)] for i in range(3)]
    bias_grad = sums[3 * gain_rows : 3 * gain_rows + bucket_rows * head_count]
    return (
        jnp.stack(layer_output),
        jnp.stack(grad_input),
        grad_states,
        gain_grads[0],
        self_q,
        self_k,
        self_v,
        self_o,
        bias_grad.reshape(bucket_rows, head_count),
        gain_grads[1],
        cross_q,
        cross_k,
        cross_v,
        cross_o,
        gain_grads[2],
        ffn_gate_grad,
        ffn_up_grad,
        ffn_down_grad,
    )


def solution(mesh):
    in_specs = (
        P("fsdp", "ctx", None),
        P("fsdp", "ctx", None),
        P("fsdp", None),
        P("fsdp", None),
        P(),
        P("fsdp", "ctx", None),
        P("fsdp"),
        P("fsdp", "tp"),
        P("fsdp", "tp"),
        P("fsdp", "tp"),
        P("tp", "fsdp"),
        P("fsdp", "tp"),
        P("fsdp"),
        P("fsdp", "tp"),
        P("fsdp", "tp"),
        P("fsdp", "tp"),
        P("tp", "fsdp"),
        P("fsdp"),
        P("fsdp", "tp"),
        P("fsdp", "tp"),
        P("tp", "fsdp"),
    )
    out_specs = (
        P("fsdp", "ctx", None),
        P("fsdp", "ctx", None),
        P("fsdp", "ctx", None),
        P("fsdp"),
        P("fsdp", "tp"),
        P("fsdp", "tp"),
        P("fsdp", "tp"),
        P("tp", "fsdp"),
        P("fsdp", "tp"),
        P("fsdp"),
        P("fsdp", "tp"),
        P("fsdp", "tp"),
        P("fsdp", "tp"),
        P("tp", "fsdp"),
        P("fsdp"),
        P("fsdp", "tp"),
        P("fsdp", "tp"),
        P("tp", "fsdp"),
    )
    return jax.shard_map(body, mesh=mesh, in_specs=in_specs, out_specs=out_specs, check_vma=False)
```

```python
import functools
import jax
import jax.numpy as jnp
from jax import lax
from jax.experimental import pallas as pl
from jax.experimental.pallas import tpu as pltpu
from jax.sharding import PartitionSpec as P

EPSILON = 1e-06
NEGATIVE = -1e30
EXTRA = 16
TINY = pl.CostEstimate(flops=1, bytes_accessed=1, transcendentals=0)
LANES = 128
STRIP = 64
CHUNK = 256
NT = (((1,), (1,)), ((), ()))
NN = (((1,), (0,)), ((), ()))


def dot(lhs, rhs, dims=NN):
    return lax.dot_general(lhs, rhs, dims, preferred_element_type=jnp.float32)


def fill_mask(mask_ref, seg_row, seg_col_ref, offset_ref, causal):
    rows = seg_row.shape[1]
    keys = mask_ref.shape[0]
    for start in range(0, keys, CHUNK):
        size = min(CHUNK, keys - start)
        seen = seg_col_ref[0, pl.ds(start, size), :] == seg_row
        if causal:
            key_place = lax.broadcasted_iota(jnp.int32, (size, rows), 0) + start
            query_place = lax.broadcasted_iota(jnp.int32, (size, rows), 1) + offset_ref[0, 0]
            seen = seen & (key_place <= query_place)
        mask_ref[pl.ds(start, size), :] = jnp.where(seen, 0.0, NEGATIVE)


def fill_bias(bias_ref, head, line):
    width = line.shape[1]
    base = jnp.broadcast_to(line, (8, width))
    row = lax.broadcasted_iota(jnp.int32, (8, width), 0)
    for bit in (1, 2, 4):
        base = jnp.where((row & bit) != 0, pltpu.roll(base, bit, 1), base)
    for block in range(LANES // 8):
        bias_ref[head, pl.ds(8 * block, 8), :] = pltpu.roll(base, 8 * block, 1) if block else base


def fold_diagonals(total):
    width = total.shape[1]
    half = total.shape[0] // 2
    while half >= 8:
        total = total[:half] + pltpu.roll(total[half:], width - half, 1)
        half //= 2
    row = lax.broadcasted_iota(jnp.int32, (8, width), 0)
    for bit in (4, 2, 1):
        total = jnp.where((row & bit) != 0, pltpu.roll(total, width - bit, 1), total)
    return jnp.sum(total, axis=0, keepdims=True)


def head_mask(rows, head):
    lane = lax.broadcasted_iota(jnp.int32, (rows, LANES), 1)
    return (lane // (LANES // 2)) == head


def add_bias(scores, bias_ref, head, start, keys, rows):
    parts = []
    for sub in range(0, scores.shape[0], LANES):
        at = keys - (start + sub)
        parts.append(scores[sub : sub + LANES] + bias_ref[head, :, at : at + rows])
    return jnp.concatenate(parts, axis=0)


def forward_kernel(causal, *refs):
    if causal:
        (offset_ref, line_ref, seg_row_ref, seg_col_ref, q_ref, k_ref, v_ref, out_ref, log_ref,
         mask_ref, score_ref, bias_ref) = refs
    else:
        (seg_row_ref, seg_col_ref, q_ref, k_ref, v_ref, out_ref, log_ref,
         mask_ref, score_ref) = refs
        offset_ref = None
    pair = pl.program_id(0)
    seq = pl.program_id(1)
    rows = q_ref.shape[1]
    keys = k_ref.shape[1]

    @pl.when(pair == 0)
    def _():
        fill_mask(mask_ref.at[seq], seg_row_ref[0], seg_col_ref, offset_ref, causal)

    if causal:

        @pl.when(seq == 0)
        def _():
            for head in range(2):
                fill_bias(bias_ref, head, line_ref[0, pl.ds(head, 1), :])

    q = q_ref[0]
    v_turned = v_ref[0].T
    half = LANES // 2
    outs = []
    logs = []
    for head in range(2):
        q_head = jnp.where(head_mask(rows, head), q, jnp.zeros_like(q))
        highest = None
        for start in range(0, keys, CHUNK):
            scores = dot(k_ref[0, pl.ds(start, CHUNK), :], q_head, NT)
            scores = scores + mask_ref[seq, pl.ds(start, CHUNK), :]
            if causal:
                scores = add_bias(scores, bias_ref, head, start, keys, rows)
            score_ref[pl.ds(start, CHUNK), :] = scores
            top = jnp.max(scores, axis=0, keepdims=True)
            highest = top if highest is None else jnp.maximum(highest, top)
        total = None
        attended = None
        for start in range(0, keys, CHUNK):
            grown = jnp.exp(score_ref[pl.ds(start, CHUNK), :] - highest)
            part = jnp.sum(grown, axis=0, keepdims=True)
            piece = dot(v_turned[half * head : half * head + half, start : start + CHUNK],
                        grown.astype(jnp.bfloat16))
            total = part if total is None else total + part
            attended = piece if attended is None else attended + piece
        outs.append(attended / total)
        logs.append(highest + jnp.log(total))
    out_ref[0] = jnp.concatenate(outs, axis=0).T.astype(jnp.bfloat16)
    log_ref[0, 0] = jnp.concatenate(logs + [jnp.zeros((6, rows), jnp.float32)], axis=0)


def backward_kernel(causal, *refs):
    if causal:
        (offset_ref, line_ref, seg_row_ref, seg_col_ref, q_ref, k_ref, v_ref, out_ref, log_ref,
         grad_ref, dq_ref, dk_ref, dv_ref, line_grad_ref, mask_ref, bias_ref, total_ref) = refs
    else:
        (seg_row_ref, seg_col_ref, q_ref, k_ref, v_ref, out_ref, log_ref,
         grad_ref, dq_ref, dk_ref, dv_ref, mask_ref) = refs
        offset_ref = None
    pair = pl.program_id(0)
    seq = pl.program_id(1)
    rows = q_ref.shape[1]
    keys = k_ref.shape[1]
    half = LANES // 2

    @pl.when(pair == 0)
    def _():
        fill_mask(mask_ref.at[seq], seg_row_ref[0], seg_col_ref, offset_ref, causal)

    if causal:

        @pl.when(seq == 0)
        def _():
            for head in range(2):
                fill_bias(bias_ref, head, line_ref[0, pl.ds(head, 1), :])
            total_ref[...] = jnp.zeros_like(total_ref)

    q = q_ref[0]
    grad = grad_ref[0]
    product = grad.astype(jnp.float32) * out_ref[0].astype(jnp.float32)
    chooser = (
        lax.broadcasted_iota(jnp.int32, (8, LANES), 1) // half
        == lax.broadcasted_iota(jnp.int32, (8, LANES), 0)
    ).astype(jnp.float32)
    inner = lax.dot_general(chooser, product, NT, precision=lax.Precision.HIGHEST,
                            preferred_element_type=jnp.float32)
    q_heads = [jnp.where(head_mask(rows, h), q, jnp.zeros_like(q)) for h in range(2)]
    grad_heads = [jnp.where(head_mask(rows, h), grad, jnp.zeros_like(grad)) for h in range(2)]
    dq = [None, None]
    for start in range(0, keys, CHUNK):
        k = k_ref[0, pl.ds(start, CHUNK), :]
        v = v_ref[0, pl.ds(start, CHUNK), :]
        k_turned = k.T
        dk = None
        dv = None
        for head in range(2):
            scores = dot(k, q_heads[head], NT)
            scores = scores + mask_ref[seq, pl.ds(start, CHUNK), :]
            if causal:
                scores = add_bias(scores, bias_ref, head, start, keys, rows)
            weights = jnp.exp(scores - log_ref[0, 0, pl.ds(head, 1), :])
            dv_part = dot(weights.astype(jnp.bfloat16), grad_heads[head])
            dw = dot(v, grad_heads[head], NT)
            ds = weights * (dw - inner[head : head + 1])
            ds_low = ds.astype(jnp.bfloat16)
            dk_part = dot(ds_low, q_heads[head])
            dq_part = dot(k_turned[half * head : half * head + half], ds_low)
            dv = dv_part if dv is None else dv + dv_part
            dk = dk_part if dk is None else dk + dk_part
            dq[head] = dq_part if dq[head] is None else dq[head] + dq_part
            if causal:
                for sub in range(0, CHUNK, LANES):
                    at = keys - (start + sub)
                    total_ref[head, :, at : at + rows] += ds[sub : sub + LANES]
        dk_ref[0, pl.ds(start, CHUNK), :] = dk.astype(jnp.bfloat16)
        dv_ref[0, pl.ds(start, CHUNK), :] = dv.astype(jnp.bfloat16)
    dq_ref[0] = jnp.concatenate(dq, axis=0).T.astype(jnp.bfloat16)
    if causal:

        @pl.when(seq == pl.num_programs(1) - 1)
        def _():
            lines = [fold_diagonals(total_ref[head]) for head in range(2)]
            lines.append(jnp.zeros((6, lines[0].shape[1]), jnp.float32))
            line_grad_ref[0] = jnp.concatenate(lines, axis=0)


def specs_for(rows, keys, pairs, causal):
    def wide(count, shift=0):
        return pl.BlockSpec((1, count, LANES), lambda p, s: (s, 0, p + shift))

    lead = []
    if causal:
        lead = [
            pl.BlockSpec((1, 1), lambda p, s: (0, 0), memory_space=pltpu.SMEM),
            pl.BlockSpec((1, 8, rows + keys), lambda p, s: (p, 0, 0)),
        ]
    lead += [
        pl.BlockSpec((1, 1, rows), lambda p, s: (s, 0, 0)),
        pl.BlockSpec((1, keys, 1), lambda p, s: (s, 0, 0)),
        wide(rows),
        wide(keys),
        wide(keys, pairs),
    ]
    return lead, wide, pl.BlockSpec((1, 1, 8, rows), lambda p, s: (s, p, 0, 0))


def attend_forward(q, kv, seg_row, seg_col, offset=None, lines=None):
    seqs, rows, width = q.shape
    keys = kv.shape[1]
    pairs = width // LANES
    causal = lines is not None
    lead, wide, logs = specs_for(rows, keys, pairs, causal)
    scratch = [pltpu.VMEM((seqs, keys, rows), jnp.float32), pltpu.VMEM((keys, rows), jnp.float32)]
    args = [seg_row, seg_col, q, kv, kv]
    if causal:
        args = [offset, lines] + args
        scratch.append(pltpu.VMEM((2, LANES, rows + keys), jnp.float32))
    return pl.pallas_call(
        functools.partial(forward_kernel, causal),
        grid=(pairs, seqs),
        in_specs=lead,
        out_specs=[wide(rows), logs],
        out_shape=[
            jax.ShapeDtypeStruct((seqs, rows, width), jnp.bfloat16),
            jax.ShapeDtypeStruct((seqs, pairs, 8, rows), jnp.float32),
        ],
        scratch_shapes=scratch,
        compiler_params=pltpu.CompilerParams(vmem_limit_bytes=16 * 1024 * 1024),
        cost_estimate=TINY,
        name="attend_forward",
    )(*args)


def attend_backward(q, kv, seg_row, seg_col, out, logs_value, grad, offset=None, lines=None):
    seqs, rows, width = q.shape
    keys = kv.shape[1]
    pairs = width // LANES
    causal = lines is not None
    lead, wide, logs = specs_for(rows, keys, pairs, causal)
    scratch = [pltpu.VMEM((seqs, keys, rows), jnp.float32)]
    args = [seg_row, seg_col, q, kv, kv, out, logs_value, grad]
    out_shape = [
        jax.ShapeDtypeStruct((seqs, rows, width), jnp.bfloat16),
        jax.ShapeDtypeStruct((seqs, keys, width), jnp.bfloat16),
        jax.ShapeDtypeStruct((seqs, keys, width), jnp.bfloat16),
    ]
    out_specs = [wide(rows), wide(keys), wide(keys)]
    if causal:
        args = [offset, lines] + args
        scratch.append(pltpu.VMEM((2, LANES, rows + keys), jnp.float32))
        scratch.append(pltpu.VMEM((2, LANES, rows + keys), jnp.float32))
        out_shape.append(jax.ShapeDtypeStruct((pairs, 8, rows + keys), jnp.float32))
        out_specs.append(pl.BlockSpec((1, 8, rows + keys), lambda p, s: (p, 0, 0)))
    return pl.pallas_call(
        functools.partial(backward_kernel, causal),
        grid=(pairs, seqs),
        in_specs=lead + [wide(rows), logs, wide(rows)],
        out_specs=out_specs,
        out_shape=out_shape,
        scratch_shapes=scratch,
        compiler_params=pltpu.CompilerParams(vmem_limit_bytes=18 * 1024 * 1024),
        cost_estimate=TINY,
        name="attend_backward",
    )(*args)


def gradient_kernel(spans, tokens, split, *refs):
    if split:
        place_ref, refs = refs[0], refs[1:]
    lhs_count = len(tokens)
    lhs_refs = refs[:lhs_count]
    seqs = (len(refs) - lhs_count - (3 if split else 2)) // len(spans)
    rhs_refs = refs[lhs_count : lhs_count + seqs * len(spans)]
    outs = refs[lhs_count + seqs * len(spans) : -1]
    turned_ref = refs[-1]
    step = pl.program_id(0)
    for index, (first, last, group) in enumerate(spans):

        @pl.when(step == first)
        def _():
            if index == 0 or spans[index - 1][2] != group:
                for s in range(seqs):
                    lhs = lhs_refs[group * seqs + s]
                    size = lhs.shape[0]
                    turned_ref[:, s * size : (s + 1) * size] = lhs[...].T

        @pl.when((step >= first) & (step < last))
        def _():
            total = None
            for s in range(seqs):
                size = lhs_refs[group * seqs + s].shape[0]
                part = dot(turned_ref[:, s * size : (s + 1) * size], rhs_refs[index * seqs + s][...])
                total = part if total is None else total + part
            if split:
                low = place_ref[0, 0]
                rows = split
                for block in range(total.shape[0] // (2 * rows)):
                    even = total[2 * block * rows : (2 * block + 1) * rows]
                    odd = total[(2 * block + 1) * rows : (2 * block + 2) * rows]
                    at = pl.ds(block * rows, rows)
                    outs[0][at, :] = jnp.where(low == 0, odd, even).astype(jnp.bfloat16)
                    outs[1][at, :] = jnp.where(low == 0, even, odd).astype(jnp.bfloat16)
            else:
                outs[0][...] = total.astype(jnp.bfloat16)


def gradient_blocks(segments, columns, place=None, split=0):
    width = segments[0][0][0].shape[1]
    lhs_args, lhs_keys, rhs_args, rhs_specs, spans, specs = [], [], [], [], [], []
    first = 0
    flops = 0
    for lhs, rhs in segments:
        count = rhs[0].shape[1] // columns
        key = tuple(id(v) for v in lhs)
        if key not in lhs_keys:
            lhs_keys.append(key)
            lhs_args.extend(lhs)
        spans.append((first, first + count, lhs_keys.index(key)))
        for value in rhs:
            flops += 2 * value.shape[0] * value.shape[1] * width

            def where(i, first=first, count=count):
                return (0, jnp.clip(i - first, 0, count - 1))

            rhs_args.append(value)
            rhs_specs.append(pl.BlockSpec((value.shape[0], columns), where))
        first += count
    for value in lhs_args:
        specs.append(pl.BlockSpec(value.shape, lambda i: (0, 0)))
    tokens = [v.shape[0] for v in lhs_args]
    longest = max(sum(v.shape[0] for v in lhs) for lhs, rhs in segments)
    out_width = first * columns
    args = lhs_args + rhs_args
    specs = specs + rhs_specs
    if split:
        args = [place] + args
        specs = [pl.BlockSpec((1, 1), lambda i: (0, 0), memory_space=pltpu.SMEM)] + specs
        shapes = [jax.ShapeDtypeStruct((width // 2, out_width), jnp.bfloat16)] * 2
        out_specs = [pl.BlockSpec((width // 2, columns), lambda i: (0, i))] * 2
    else:
        shapes = jax.ShapeDtypeStruct((width, out_width), jnp.bfloat16)
        out_specs = pl.BlockSpec((width, columns), lambda i: (0, i))
    return pl.pallas_call(
        functools.partial(gradient_kernel, spans, tokens, split),
        grid=(first,),
        in_specs=specs,
        out_specs=out_specs,
        out_shape=shapes,
        scratch_shapes=[pltpu.VMEM((width, longest), jnp.bfloat16)],
        compiler_params=pltpu.CompilerParams(vmem_limit_bytes=36 * 1024 * 1024),
        cost_estimate=TINY,
        name="weight_gradients",
    )(*args)


def mm(lhs, rhs):
    return dot(lhs, rhs)


def mm_back(lhs, rhs):
    return dot(lhs, rhs, NT)


def rms_forward(values, gain_row):
    inverse_rms = lax.rsqrt(jnp.mean(values * values, axis=-1, keepdims=True) + EPSILON)
    unit_rows = values * inverse_rms
    return unit_rows, inverse_rms, (unit_rows * gain_row).astype(jnp.bfloat16)


def rms_backward(grad_normed, unit_rows, inverse_rms, gain_row):
    grad_unit = grad_normed * gain_row
    grad_gain = jnp.sum(grad_normed * unit_rows, axis=0)
    inner_sum = jnp.mean(grad_unit * unit_rows, axis=-1, keepdims=True)
    return inverse_rms * (grad_unit - unit_rows * inner_sum), grad_gain


def low_cast(value):
    return value.astype(jnp.bfloat16)


def wide_cast(value):
    return value.astype(jnp.float32)


def ctx_shape():
    count = lax.axis_size("ctx")
    low = 2 if count % 2 == 0 else 1
    return count // low, low


def ctx_place():
    high, low = ctx_shape()
    index = lax.axis_index("ctx")
    return index // low, index % low


def swap_low(value):
    high, low = ctx_shape()
    return lax.ppermute(value, "ctx", [(i, i ^ 1) for i in range(high * low)])


def shift_high(value, step, wrap):
    high, low = ctx_shape()
    pairs = []
    for i in range(high * low):
        target = i // low + step
        if wrap or 0 <= target < high:
            pairs.append((i, (target % high) * low + i % low))
    return lax.ppermute(value, "ctx", pairs)


def shift_fsdp(value, step):
    count = lax.axis_size("fsdp")
    return lax.ppermute(value, "fsdp", [(i, (i + step) % count) for i in range(count)])


def put(buffer, value, at, axis):
    return lax.dynamic_update_slice_in_dim(buffer, jnp.expand_dims(value, axis), at, axis)


def ctx_gather(value, causal, axis, earlier):
    high, low = ctx_shape()
    at_high, at_low = ctx_place()
    pieces = [value] + [shift_high(value, step, not causal) for step in range(1, high)]
    pieces = before(pieces, earlier)
    places = [((at_high - step) % high, at_low) for step in range(high)]
    if low == 2:
        pieces = pieces + [swap_low(piece) for piece in pieces]
        places = places + [((at_high - step) % high, 1 - at_low) for step in range(high)]
    shape = value.shape[:axis] + (high, low) + value.shape[axis:]
    held = assemble(pieces, places, shape, axis)
    shape = value.shape[:axis] + (high * low * value.shape[axis],) + value.shape[axis + 1 :]
    return held.reshape(shape)


def gather_rows(shards, earlier):
    count = lax.axis_size("ctx")
    rows = shards[0].shape[0] // count
    start = lax.axis_index("ctx") * rows
    shards = before(shards, earlier)
    parts = [lax.dynamic_slice_in_dim(s, start, rows, 0) for s in shards]
    part = jnp.concatenate(parts, axis=1) if len(parts) > 1 else parts[0]
    return lax.all_gather(part, ("fsdp", "ctx"), axis=0, tiled=True)


def before(value, *earlier):
    return lax.optimization_barrier((value, earlier))[0]


def assemble_kernel(lead, place_ref, *refs):
    pieces, out_ref = refs[:-1], refs[-1]
    step = pl.program_id(0)
    for index, piece in enumerate(pieces):

        @pl.when(step == index)
        def _():
            rows = out_ref.shape[-2]
            out_ref[...] = piece[..., :rows, :].reshape(out_ref.shape)


def assemble(pieces, places, shape, lead):
    places = jnp.stack([jnp.stack([jnp.asarray(v, jnp.int32) for v in p]) for p in places])
    block = shape[:lead] + (1, 1) + shape[lead + 2 :]
    rank = len(pieces[0].shape)

    def where(i, place):
        return (0,) * lead + (place[i, 0], place[i, 1]) + (0,) * (len(shape) - lead - 2)

    return pl.pallas_call(
        functools.partial(assemble_kernel, lead),
        grid_spec=pltpu.PrefetchScalarGridSpec(
            num_scalar_prefetch=1,
            grid=(len(pieces),),
            in_specs=[pl.BlockSpec(p.shape, lambda i, place: (0,) * rank) for p in pieces],
            out_specs=pl.BlockSpec(block, where),
        ),
        out_shape=jax.ShapeDtypeStruct(shape, pieces[0].dtype),
        compiler_params=pltpu.CompilerParams(vmem_limit_bytes=16 * 1024 * 1024),
        cost_estimate=TINY,
        name="assemble",
    )(places, *pieces)


def first_part(shards):
    high, low = ctx_shape()
    at_high, at_low = ctx_place()
    rows = shards[0].shape[0] // low
    parts = [lax.dynamic_slice_in_dim(s, at_low * rows, rows, 0) for s in shards]
    return jnp.concatenate(parts, axis=1) if len(parts) > 1 else parts[0]


def first_pieces(part):
    count = lax.axis_size("fsdp")
    if count > 8:
        held = lax.all_gather(part, "fsdp", axis=0, tiled=False)
        index = lax.axis_index("fsdp")
        return [
            lax.dynamic_index_in_dim(held, (index - step) % count, 0, False)
            for step in range(count)
        ]
    return [part] + [shift_fsdp(part, step) for step in range(1, count)]


def first_whole(pieces, rows):
    count = lax.axis_size("fsdp")
    index = lax.axis_index("fsdp")
    high, low = ctx_shape()
    at_high, at_low = ctx_place()
    columns = pieces[0].shape[1]
    places = [((index - step) % count, at_low) for step in range(count)]
    if low == 2:
        pieces = pieces + [swap_low(piece) for piece in pieces]
        places = places + [((index - step) % count, 1 - at_low) for step in range(count)]
    whole = assemble(pieces, places, (count, low, rows, columns), 0)
    return whole.reshape(count * low * rows, columns)


def gather_small(value):
    count = lax.axis_size("fsdp")
    index = lax.axis_index("fsdp")
    if count > 8:
        return lax.all_gather(value, "fsdp", axis=0, tiled=False)
    held = put(jnp.zeros((count,) + value.shape, value.dtype), value, index, 0)
    for step in range(1, count):
        held = put(held, shift_fsdp(value, step), (index - step) % count, 0)
    return held


def fold_start(segments, columns, arrive=None):
    high, low = ctx_shape()
    at_high, at_low = ctx_place()
    count = lax.axis_size("fsdp")
    width = segments[0][0][0].shape[1]
    rows = width // (count * high * low)
    shape = (count, high, rows, -1)
    if low == 2:
        place = jnp.full((1, 1), at_low, jnp.int32)
        away, kept = gradient_blocks(segments, columns, place, rows)
        done = away
        if arrive is not None:
            arrive, away = before((arrive, away), away)
            done = (arrive, done)
        return [kept.reshape(shape), swap_low(away).reshape(shape)], done
    kept = gradient_blocks(segments, columns)
    return [kept.reshape(shape)], kept if arrive is None else (before(arrive, kept), kept)


def fold_high(parts, earlier=()):
    high, low = ctx_shape()
    at_high, at_low = ctx_place()
    parts = before(parts, earlier)
    found, sent = [], []
    for step in range(1, high):
        mine, piece = split_sum(parts, [at_high, (at_high + step) % high])
        found = found or [mine]
        sent.append(piece)
        found.append(shift_high(piece, step, True))
    return found, (found[0], sent)


def fold_fsdp(parts, lines, earlier=()):
    count = lax.axis_size("fsdp")
    index = lax.axis_index("fsdp")
    parts, lines = before((parts, lines), earlier)
    small = jnp.zeros((count, EXTRA, parts[0].shape[2]), jnp.bfloat16)
    small = small.at[:, 0, : lines.shape[1]].set(low_cast(lines))
    if count > 8:
        whole = low_cast(sum(wide_cast(p) for p in parts))
        whole = jnp.concatenate([whole, small], axis=1)
        flat = whole.reshape((-1,) + whole.shape[2:])
        return [lax.psum_scatter(flat, "fsdp", scatter_dimension=0, tiled=True)], whole

    def part(at):
        total = sum(wide_cast(lax.dynamic_index_in_dim(p, at, 0, False)) for p in parts)
        line = lax.dynamic_index_in_dim(small, at, 0, False)
        return jnp.concatenate([low_cast(total), line], axis=0)

    sent = [part((index + step) % count) for step in range(1, count)]
    mine = part(index)
    moved = [shift_fsdp(piece, step + 1) for step, piece in enumerate(sent)]
    return [mine] + moved, (mine, sent)


def fold_fsdp_first(halves, earlier=()):
    count = lax.axis_size("fsdp")
    index = lax.axis_index("fsdp")
    halves = before(halves, earlier)
    if count > 8:
        whole = low_cast(sum(wide_cast(h) for h in halves))
        flat = whole.reshape((-1,) + whole.shape[2:])
        part = lax.psum_scatter(flat, "fsdp", scatter_dimension=0, tiled=True)
        return [part.reshape(whole.shape[1:])], whole

    def part(at):
        return low_cast(sum(wide_cast(lax.dynamic_index_in_dim(h, at, 0, False)) for h in halves))

    sent = [part((index + step) % count) for step in range(1, count)]
    mine = part(index)
    moved = [shift_fsdp(piece, step + 1) for step, piece in enumerate(sent)]
    return [mine] + moved, (mine, sent)


def fold_high_last(parts, earlier=()):
    high, low = ctx_shape()
    at_high, at_low = ctx_place()
    parts = before(parts, earlier)

    def part(at):
        return low_cast(sum(wide_cast(lax.dynamic_index_in_dim(p, at, 0, False)) for p in parts))

    sent = [part((at_high + step) % high) for step in range(1, high)]
    mine = part(at_high)
    moved = [shift_high(piece, step + 1, True) for step, piece in enumerate(sent)]
    return [mine] + moved, (mine, sent)


def swap_fsdp(value, bit):
    count = lax.axis_size("fsdp")
    return lax.ppermute(value, "fsdp", [(i, i ^ bit) for i in range(count)])


def doubles(count):
    return count <= 8 and count & (count - 1) == 0


def fold_fsdp_start(parts, lines=None, earlier=(), hold=()):
    count = lax.axis_size("fsdp")
    index = lax.axis_index("fsdp")
    parts, lines = before((parts, lines), earlier)
    rest = parts[0].shape[1:]
    small = None
    if lines is not None:
        small = jnp.zeros((count, EXTRA, rest[-1]), jnp.bfloat16)
        small = small.at[:, 0, : lines.shape[1]].set(low_cast(lines))
    if not doubles(count):
        whole = low_cast(sum(wide_cast(p) for p in parts))
        if small is not None:
            whole = jnp.concatenate([whole, small], axis=1)
        flat = whole.reshape((-1,) + whole.shape[2:])
        part = lax.psum_scatter(flat, "fsdp", scatter_dimension=0, tiled=True)
        return [part.reshape((1,) + whole.shape[1:])], whole
    views = [p.reshape((count // 2, 2) + (-1, rest[-1])) for p in parts]
    if small is not None:
        small = small.reshape(count // 2, 2, EXTRA, rest[-1])
    mine, sent = split_sum(views, [index % 2, 1 - index % 2], small)
    shape = (count // 2,) + (rest if small is None else mine.shape[1:])
    return [mine.reshape(shape), swap_fsdp(before(sent, hold), 1).reshape(shape)], (mine, sent)


def fold_fsdp_rest(parts, earlier=()):
    count = lax.axis_size("fsdp")
    index = lax.axis_index("fsdp")
    parts = before(parts, earlier)
    done = parts[0]
    bit = 2
    while doubles(count) and bit < count:
        rest = parts[0].shape[1:]
        views = [p.reshape((p.shape[0] // 2, 2) + (-1, rest[-1])) for p in parts]
        at = (index // bit) % 2
        mine, sent = split_sum(views, [at, 1 - at])
        done = (mine, sent)
        parts = [v.reshape((-1,) + rest) for v in (mine, swap_fsdp(sent, bit))]
        bit *= 2
    return parts, done


def fold_own(parts, earlier=()):
    parts = before(parts, earlier)
    total = add_parts(parts) if len(parts) > 1 else parts[0]
    return total.reshape(-1, total.shape[-1])


def spread_high(part):
    high, low = ctx_shape()
    return [part] + [shift_high(part, step, True) for step in range(1, high)]


def spread_low(parts, earlier=()):
    high, low = ctx_shape()
    parts = before(parts, earlier)
    return parts, [swap_low(p) if low == 2 else p for p in parts]


def finish_kernel(high, low, cuts, extra, place_ref, *refs):
    mine_refs, other_refs, outs = refs[:high], refs[high : 2 * high], refs[2 * high :]
    rows = mine_refs[0].shape[0] - extra

    def chosen(at_high, at_low, start, stop):
        step = lax.rem(place_ref[0, 0] - at_high + high, high)
        value = None
        for index in range(high):
            mine = mine_refs[index][:rows, start:stop]
            other = other_refs[index][:rows, start:stop]
            piece = jnp.where(place_ref[0, 1] == at_low, mine, other)
            value = piece if value is None else jnp.where(step == index, piece, value)
        return wide_cast(value)

    for (start, stop, turned), out in zip(cuts, outs):
        blocks = [chosen(h, l, start, stop) for h in range(high) for l in range(low)]
        if turned:
            out[...] = jnp.concatenate(blocks, axis=0).T
        else:
            for index, block in enumerate(blocks):
                out[pl.ds(index * rows, rows), :] = block
    if extra:
        total = None
        for ref in mine_refs + (other_refs if low == 2 else ()):
            line = wide_cast(ref[rows:, :])
            total = line if total is None else total + line
        outs[-1][...] = total


def spread_end(pair, cuts, extra=0):
    high, low = ctx_shape()
    at_high, at_low = ctx_place()
    mine, other = pair
    rows = mine[0].shape[0] - extra
    shapes = []
    for start, stop, turned in cuts:
        shape = (high * low * rows, stop - start)
        shapes.append(jax.ShapeDtypeStruct(shape[::-1] if turned else shape, jnp.float32))
    if extra:
        shapes.append(jax.ShapeDtypeStruct((extra, mine[0].shape[1]), jnp.float32))
    place = jnp.stack([at_high, at_low]).astype(jnp.int32).reshape(1, 2)
    vmem = pl.BlockSpec(memory_space=pltpu.VMEM)
    return pl.pallas_call(
        functools.partial(finish_kernel, high, low, cuts, extra),
        in_specs=[pl.BlockSpec(memory_space=pltpu.SMEM)] + [vmem] * (2 * high),
        out_specs=[vmem] * len(shapes),
        out_shape=shapes,
        compiler_params=pltpu.CompilerParams(vmem_limit_bytes=20 * 1024 * 1024),
        cost_estimate=TINY,
        name="finish",
    )(place, *mine, *other)


def block_fold_start(lefts, rights):
    high, low = ctx_shape()
    at_high, at_low = ctx_place()
    size = lefts[0].shape[0] // (high * low)

    def part(at):
        views = [v.reshape(high, low, size, -1) for v in lefts + rights]
        views = [lax.dynamic_index_in_dim(v, at, 1, False) for v in views]
        views = [
            jnp.concatenate([views[i], views[len(lefts) + i]], axis=-1) for i in range(len(lefts))
        ]
        return jnp.concatenate(views, axis=1) if len(views) > 1 else views[0]

    if low == 1:
        whole = part(0)
        return [whole], whole
    away = part(1 - at_low)
    kept = part(at_low)
    return [kept, swap_low(away)], (kept, away)


def block_fold_high(halves, causal, earlier=()):
    high, low = ctx_shape()
    at_high, at_low = ctx_place()
    halves = before(halves, earlier)

    def part(at):
        return low_cast(sum(wide_cast(lax.dynamic_index_in_dim(h, at, 0, False)) for h in halves))

    sent = [part((at_high - step) % high) for step in range(1, high)]
    mine = part(at_high)
    moved = [shift_high(piece, -step - 1, not causal) for step, piece in enumerate(sent)]
    return [mine] + moved, (mine, sent)


def block_fold_end(parts, earlier=()):
    parts = before(parts, earlier)
    return low_cast(sum(wide_cast(p) for p in parts))


def norm_backward(parts, rest_ref, values_ref, gain_ref, out_ref, low_ref, gain_out_ref):
    gain = wide_cast(gain_ref[...])
    total = jnp.zeros((8, gain.shape[1]), jnp.float32)
    for start in range(0, rest_ref.shape[0], STRIP):
        at = pl.ds(start, STRIP)
        unit, inverse, normed = rms_rows(wide_cast(values_ref[at, :]), gain)
        grad = sum(wide_cast(p[at, :]) for p in parts)
        product = grad * unit
        for row in range(0, STRIP, 8):
            total = total + product[row : row + 8]
        inner = jnp.mean(product * gain, axis=1, keepdims=True)
        result = wide_cast(rest_ref[at, :]) + inverse * (grad * gain - unit * inner)
        if out_ref is not None:
            out_ref[at, :] = result
        low_ref[at, :] = low_cast(result)
    gain_out_ref[...] = total


def rms_rows(values, gain):
    inverse = lax.rsqrt(jnp.mean(values * values, axis=1, keepdims=True) + EPSILON)
    unit = values * inverse
    return unit, inverse, low_cast(unit * gain)


def project_end_kernel(mine_ref, moved_ref, dq_ref, wide_ref, own_ref):
    width = dq_ref.shape[1]
    folded = low_cast(wide_cast(mine_ref[...]) + wide_cast(moved_ref[...]))
    for start in range(0, own_ref.shape[1], CHUNK):
        at = pl.ds(start, CHUNK)
        total = dot(dq_ref[...], wide_ref[at, :width], NT)
        own_ref[:, at] = low_cast(total + dot(folded, wide_ref[at, width:], NT))


def project_end(parts, dq, wide_weights):
    vmem = pl.BlockSpec(memory_space=pltpu.VMEM)
    return pl.pallas_call(
        project_end_kernel,
        in_specs=[vmem] * 4,
        out_specs=vmem,
        out_shape=jax.ShapeDtypeStruct((dq.shape[0], wide_weights.shape[0]), jnp.bfloat16),
        compiler_params=pltpu.CompilerParams(vmem_limit_bytes=16 * 1024 * 1024),
        cost_estimate=TINY,
        name="project_end",
    )(parts[0], parts[1], dq, wide_weights)


def last_norm_kernel(part_ref, moved_ref, rest_ref, values_ref, gain_ref, low_ref, gain_out_ref):
    norm_backward([part_ref, moved_ref], rest_ref, values_ref, gain_ref, None, low_ref,
                  gain_out_ref)


def last_norm(parts, rest, values, gain):
    vmem = pl.BlockSpec(memory_space=pltpu.VMEM)
    return pl.pallas_call(
        last_norm_kernel,
        in_specs=[vmem] * 5,
        out_specs=[vmem] * 2,
        out_shape=[jax.ShapeDtypeStruct(rest.shape, jnp.bfloat16), jax.ShapeDtypeStruct((8, rest.shape[1]), jnp.float32)],
        compiler_params=pltpu.CompilerParams(vmem_limit_bytes=16 * 1024 * 1024),
        cost_estimate=TINY,
        name="last_norm",
    )(parts[0], parts[1], rest, values, gain)


def add_kernel(count, *refs):
    total = sum(wide_cast(r[...]) for r in refs[:count])
    refs[count][...] = low_cast(total)


def add_parts(parts):
    vmem = pl.BlockSpec(memory_space=pltpu.VMEM)
    return pl.pallas_call(
        functools.partial(add_kernel, len(parts)),
        in_specs=[vmem] * len(parts),
        out_specs=vmem,
        out_shape=jax.ShapeDtypeStruct(parts[0].shape, jnp.bfloat16),
        compiler_params=pltpu.CompilerParams(vmem_limit_bytes=16 * 1024 * 1024),
        cost_estimate=TINY,
        name="add_parts",
    )(*parts)


def split_sum(parts, places, extra=None):
    shape = parts[0].shape
    rest = (0,) * (len(shape) - 2)
    places = jnp.stack([jnp.asarray(v, jnp.int32) for v in places])
    specs = []
    for which in range(2):
        for part in parts:
            if len(part.shape) == len(shape):
                spec = pl.BlockSpec(
                    (1, 1) + shape[2:], lambda i, place, which=which: (i, place[which]) + rest
                )
            else:
                spec = pl.BlockSpec(
                    (1, 1, 1) + shape[2:],
                    lambda i, place, which=which: (i, place[which], place[2]) + rest,
                )
            specs.append(spec)
    args = list(parts) + list(parts)
    added = 0
    if extra is not None:
        added = extra.shape[2]
        args += [extra, extra]
        for which in range(2):
            specs.append(
                pl.BlockSpec(
                    (1, 1) + extra.shape[2:],
                    lambda i, place, which=which: (i, place[which]) + rest,
                )
            )
    out_shape = (shape[2] + added,) + shape[3:]
    out = jax.ShapeDtypeStruct((shape[0],) + out_shape, jnp.bfloat16)
    out_spec = pl.BlockSpec((1,) + out_shape, lambda i, place: (i,) + rest)

    def kernel(place_ref, *refs):
        for which in range(2):
            total = None
            for ref in refs[which * len(parts) : (which + 1) * len(parts)]:
                value = wide_cast(ref[...]).reshape(shape[2:])
                total = value if total is None else total + value
            out_ref = refs[len(args) + which]
            out_ref[0, : shape[2]] = low_cast(total)
            if added:
                out_ref[0, shape[2] :] = refs[2 * len(parts) + which][0, 0]

    return pl.pallas_call(
        kernel,
        grid_spec=pltpu.PrefetchScalarGridSpec(
            num_scalar_prefetch=1,
            grid=(shape[0],),
            in_specs=specs,
            out_specs=[out_spec, out_spec],
        ),
        out_shape=[out, out],
        compiler_params=pltpu.CompilerParams(vmem_limit_bytes=16 * 1024 * 1024),
        cost_estimate=TINY,
        name="split_sum",
    )(places, *args)


def pair_start(partial):
    own = low_cast(partial)
    count = lax.axis_size("tp")
    moved = [
        lax.ppermute(own, "tp", [(i, (i + step) % count) for i in range(count)])
        for step in range(1, count)
    ]
    return [own] + moved, own


def pair_end(parts, earlier=()):
    parts = before(parts, earlier)
    return sum(wide_cast(p) for p in parts)


def body(
    hidden_in,
    encoder_states,
    dec_segments,
    enc_segments,
    bucket_table,
    out_cotangent,
    self_gain,
    self_query,
    self_key,
    self_value,
    self_output,
    position_bias,
    cross_gain,
    cross_query,
    cross_key,
    cross_value,
    cross_output,
    ffn_gain,
    ffn_gate,
    ffn_up,
    ffn_down,
):
    shards = lax.axis_size("fsdp")
    seqs, row_count, width = hidden_in.shape
    length = dec_segments.shape[1]
    hw = self_query.shape[1]
    units = ffn_gate.shape[1]
    bucket_rows, head_count = position_bias.shape
    bucket_count = bucket_rows * shards
    gain_rows = self_gain.shape[0]
    offset = lax.axis_index("ctx") * row_count
    every = range(seqs)
    last = seqs - 1

    small = jnp.concatenate([self_gain, cross_gain, ffn_gain, position_bias.reshape(-1)])
    line = jnp.zeros((EXTRA, 3 * hw), jnp.bfloat16).at[0, : small.shape[0]].set(small)
    qkv_part = first_part([self_query, self_key, self_value])
    first_rows = qkv_part.shape[0]
    qkv_part = jnp.concatenate([qkv_part, line], axis=0)
    first_arrived = first_pieces(qkv_part)
    shard = lax.axis_index("fsdp")
    small = jnp.stack([piece[first_rows, : small.shape[0]] for piece in first_arrived])
    small = jnp.stack(
        [lax.dynamic_index_in_dim(small, (shard - i) % shards, 0, False) for i in range(shards)]
    )
    gain_self, gain_cross, gain_ffn = [
        wide_cast(small[:, gain_rows * i : gain_rows * (i + 1)].reshape(width)) for i in range(3)
    ]
    bias_table = wide_cast(small[:, 3 * gain_rows :].reshape(bucket_count, head_count))
    first_weights = first_whole(first_arrived, first_rows)
    hidden_all = ctx_gather(before(hidden_in, qkv_part), True, 1, first_arrived[-1])
    source = [wide_cast(hidden_in[s]) for s in every]
    norm_one = [rms_forward(source[s], gain_self) for s in every]
    norm_all = [rms_forward(wide_cast(hidden_all[s]), gain_self)[2] for s in every]
    middle_weights = gather_rows(
        [self_output.T, cross_query, cross_key, cross_value, cross_output.T], qkv_part
    )
    gate_up = gather_rows([ffn_gate, ffn_up], qkv_part)
    ffn_down, encoder_states = before((ffn_down, encoder_states), first_weights, norm_all[0])
    down_pieces = first_pieces(first_part([ffn_down.T]))
    query_self = first_weights[:, :hw]
    pair_self = first_weights[:, hw:]
    output_self = middle_weights[:, :hw]
    query_cross = middle_weights[:, hw : 2 * hw]
    pair_cross = middle_weights[:, 2 * hw : 4 * hw]
    output_cross = middle_weights[:, 4 * hw :]

    query_docs = lax.dynamic_slice_in_dim(dec_segments, offset, row_count, 1)[:, None, :]
    dec_docs = dec_segments[:, :, None]
    enc_docs = enc_segments[:, :, None]
    bucket_onehot = wide_cast(
        bucket_table[:, None] == jnp.arange(bucket_count, dtype=jnp.int32)[None, :]
    )
    distance_bias = jnp.dot(bucket_onehot, bias_table, precision=lax.Precision.HIGHEST).T
    padded = jnp.concatenate([jnp.zeros_like(distance_bias), distance_bias], axis=1)
    lines = lax.dynamic_slice_in_dim(padded, offset, row_count + length, 1)
    lines = lines.reshape(head_count // 2, 2, row_count + length)
    lines = jnp.concatenate(
        [lines, jnp.zeros((head_count // 2, 6, row_count + length), jnp.float32)], axis=1
    )
    place = jnp.full((1, 1), offset, jnp.int32)

    def one(value, s):
        return value[s : s + 1]

    q_one, kv_one, att_one, log_one, pair_one, done = [], [], [], [], [], ()
    for s in every:
        rows_all, rows_own = before((norm_all[s], norm_one[s][2]), done)
        kv_one.append(low_cast(mm(rows_all, pair_self)))
        q_one.append(low_cast(mm(rows_own, query_self)))
        out, logs = attend_forward(
            q_one[s][None], kv_one[s][None], one(query_docs, s), one(dec_docs, s), place, lines
        )
        att_one.append(out)
        log_one.append(logs)
        rows = before(out[0], pair_one[-1]) if s else out[0]
        parts, done = pair_start(mm_back(rows, output_self))
        pair_one.append(parts)

    encoder_all = ctx_gather(encoder_states, False, 1, done)
    down = first_whole(before(down_pieces, done), down_pieces[0].shape[0])
    kv_two = [low_cast(mm(before(encoder_all[s], down), pair_cross)) for s in every]
    after_one, norm_two, q_two, att_two, log_two, pair_two = [], [], [], [], [], []
    done = (done, kv_two)
    for s in every:
        after_one.append(source[s] + pair_end(pair_one[s], done))
        norm_two.append(rms_forward(after_one[s], gain_cross))
        q_two.append(low_cast(mm(norm_two[s][2], query_cross)))
        out, logs = attend_forward(
            q_two[s][None], kv_two[s][None], one(query_docs, s), one(enc_docs, s)
        )
        att_two.append(out)
        log_two.append(logs)
        rows = out[0] if s else before(out[0], pair_one[-1])
        parts, done = pair_start(mm_back(rows, output_cross))
        pair_two.append(parts)

    grad_units = [mm(before(out_cotangent[s], done), down) for s in every]
    after_two, norm_three, units_out, grads_gate, grads_up, pair_three = [], [], [], [], [], []
    done = (done, grad_units)
    for s in every:
        after_two.append(after_one[s] + pair_end(pair_two[s], done))
        norm_three.append(rms_forward(after_two[s], gain_ffn))
        both_rows = mm(norm_three[s][2], gate_up)
        up_rows = both_rows[:, units:]
        activated, gelu_pull = jax.vjp(
            lambda v: jax.nn.gelu(v, approximate=True), both_rows[:, :units]
        )
        units_out.append(low_cast(activated * up_rows))
        grads_gate.append(low_cast(gelu_pull(grad_units[s] * up_rows)[0]))
        grads_up.append(low_cast(grad_units[s] * activated))
        parts, done = pair_start(
            mm_back(grads_gate[s], gate_up[:, :units]) + mm_back(grads_up[s], gate_up[:, units:])
        )
        pair_three.append(parts)
    cotangent = [out_cotangent[s] for s in every]
    low_three = [n[2] for n in norm_three]
    ffn_blocks = gradient_blocks(
        [
            (before(low_three, done, pair_three[0]), grads_gate),
            (low_three, grads_up),
            (cotangent, units_out),
        ],
        units,
    )
    ffn_part = lax.psum_scatter(ffn_blocks, ("fsdp", "ctx"), scatter_dimension=0, tiled=True)

    res_two, low_two, dq_two, dk_two, dv_two, gain_three, pair_four = [], [], [], [], [], [], []
    done = (done, ffn_blocks)
    for s in every:
        grad_from, gain = rms_backward(
            pair_end(pair_three[s], done), norm_three[s][0], norm_three[s][1], gain_ffn
        )
        gain_three.append(gain)
        res_two.append(wide_cast(out_cotangent[s]) + grad_from)
        low_two.append(low_cast(res_two[s]))
        grad_attended = low_cast(mm(low_two[s], output_cross))
        dq, dk, dv = attend_backward(
            q_two[s][None], kv_two[s][None], one(query_docs, s), one(enc_docs, s),
            att_two[s], log_two[s], grad_attended[None],
        )
        dq_two.append(dq[0])
        dk_two.append(dk[0])
        dv_two.append(dv[0])
        rows = before(dq[0], pair_four[-1]) if s else dq[0]
        parts, done = pair_start(mm_back(rows, query_cross))
        pair_four.append(parts)
    encoder_rows = [encoder_all[s] for s in every]
    pair_out = []
    parts, done = pair_start(mm_back(before(units_out[0], done), down))
    pair_out.append(parts)
    middle, done = fold_start(
        [
            (before([n[2] for n in norm_two], done), dq_two),
            (encoder_rows, dk_two),
            (encoder_rows, dv_two),
            (low_two, [a[0] for a in att_two]),
        ],
        hw,
    )

    res_one, low_one, dq_one, dk_one, dv_one, gain_two, line_grads, folds = (
        [], [], [], [], [], [], [], [],
    )
    encoder_fold, done = block_fold_start(before(dk_two, done), dv_two)
    layer_output = []

    def finish_output(s, earlier):
        layer_output.append(low_cast(after_two[s] + pair_end(pair_out[s], earlier)))
        return layer_output[-1]

    for s in every:
        grad_from, gain = rms_backward(
            pair_end(pair_four[s], done), norm_two[s][0], norm_two[s][1], gain_cross
        )
        gain_two.append(gain)
        res_one.append(res_two[s] + grad_from)
        low_one.append(low_cast(res_one[s]))
        grad_attended = low_cast(mm(low_one[s], output_self))
        if s == 0:
            encoder_fold, done = block_fold_high(encoder_fold, False, grad_attended)
            done = finish_output(0, done)
        else:
            folds[s - 1], done = block_fold_high(folds[s - 1], True, grad_attended)
            parts, done = pair_start(mm_back(before(units_out[s], done), down))
            pair_out.append(parts)
        dq, dk, dv, line = attend_backward(
            q_one[s][None], kv_one[s][None], one(query_docs, s), one(dec_docs, s),
            att_one[s], log_one[s], before(grad_attended, done)[None], place, lines,
        )
        dq_one.append(dq[0])
        dk_one.append(dk[0])
        dv_one.append(dv[0])
        line_grads.append(line)
        if s == 0:
            folded = block_fold_end(encoder_fold, dk)
            pair_states, own = pair_start(mm_back(folded, pair_cross))
            done = own
        if s < last:
            fold, done = block_fold_start(before([dk[0]], done), [dv[0]])
            folds.append(fold)

    first, done = fold_start(
        [
            (before(low_one, dk_one[last]), [a[0] for a in att_one]),
            ([n[2] for n in norm_one], dq_one),
        ],
        hw,
    )
    arrived = before((folds, pair_out[1:]), done)
    folds, pair_out[1:] = arrived
    fold, done = block_fold_start(before([dk_one[last]], arrived), [dv_one[last]])
    pair_six = []
    for s in range(last):
        parts, done = pair_start(project_end(before(folds[s], done), dq_one[s], first_weights))
        pair_six.append(parts)
    fold, done = block_fold_high(fold, True, done)
    second, (arrived, done) = fold_start(
        [(before(norm_all, done), dk_one), (norm_all, dv_one)], hw, (fold, pair_six)
    )
    fold, pair_six = arrived
    middle, done = fold_fsdp_start(middle, None, done, ffn_part)
    ffn_spread = spread_high(before(ffn_part, done))
    parts, done = pair_start(
        project_end(before(fold, arrived, ffn_spread[0]), dq_one[last], first_weights)
    )
    pair_six.append(parts)
    second, done = fold_high(second, done)
    first, done = fold_fsdp_start(first, None, done)
    grad_input, gain_one = [], []

    gain_row = gain_self.reshape(1, -1)

    def finish_sequence(s, earlier):
        rows, gain = last_norm(
            before(pair_six[s], earlier), res_one[s], hidden_in[s], gain_row
        )
        gain_one.append(jnp.sum(gain, axis=0))
        grad_input.append(rows)
        return rows

    for s in range(last):
        done = finish_sequence(s, done)
    middle, done = fold_fsdp_rest(middle, done)
    line_grads = before(line_grads, done)
    for s in range(1, seqs):
        done = finish_output(s, done)
    ffn_spread = spread_low(ffn_spread, done)
    second = before(second, done)
    done = finish_sequence(last, second)
    line_total = sum(line_grads)[:, :2].reshape(head_count, row_count + length)
    spread = lax.dynamic_update_slice_in_dim(
        jnp.zeros((head_count, 2 * length), jnp.float32), line_total, offset, 1
    )[:, length:]
    grad_bias = jnp.dot(spread, bucket_onehot, precision=lax.Precision.HIGHEST).T
    totals = [sum(g).reshape(shards, gain_rows) for g in (gain_one, gain_two, gain_three)]
    totals = jnp.concatenate(totals + [grad_bias.reshape(shards, -1)], axis=1)
    second, done = fold_fsdp_start(second, totals, grad_input)
    first, done = fold_fsdp_rest(first, done)
    second, done = fold_fsdp_rest(second, done)
    middle, done = fold_high(middle, done)
    first, done = fold_high(first, done)
    middle_sum = fold_own(middle, done)
    middle_spread = spread_high(middle_sum)
    second_sum = fold_own(second, middle_sum)
    done = second_sum
    ffn_gate_grad, ffn_up_grad, ffn_down_grad = spread_end(
        before(ffn_spread, done),
        [(0, units, False), (units, 2 * units, False), (2 * units, 3 * units, True)],
    )
    middle_spread = spread_low(middle_spread, ffn_gate_grad)
    first_sum = fold_own(first, middle_spread[0])
    inner = jnp.concatenate([jnp.pad(first_sum, ((0, EXTRA), (0, 0))), second_sum], axis=1)
    inner = spread_high(inner)
    cross_q, cross_k, cross_v, cross_o = spread_end(
        before(middle_spread, inner[0]),
        [(0, hw, False), (hw, 2 * hw, False), (2 * hw, 3 * hw, False), (3 * hw, 4 * hw, True)],
    )
    inner = spread_low(inner, cross_q)
    grad_states = low_cast(pair_end(pair_states, inner[0])).reshape(seqs, -1, width)
    self_o, self_q, self_k, self_v, sums = spread_end(
        inner,
        [(0, hw, True), (hw, 2 * hw, False), (2 * hw, 3 * hw, False), (3 * hw, 4 * hw, False)],
        EXTRA,
    )
    sums = sums[0, 2 * hw :]
    gain_grads = [sums[gain_rows * i : gain_rows * (i + 1)] for i in range(3)]
    bias_grad = sums[3 * gain_rows : 3 * gain_rows + bucket_rows * head_count]
    return (
        jnp.stack(layer_output),
        jnp.stack(grad_input),
        grad_states,
        gain_grads[0],
        self_q,
        self_k,
        self_v,
        self_o,
        bias_grad.reshape(bucket_rows, head_count),
        gain_grads[1],
        cross_q,
        cross_k,
        cross_v,
        cross_o,
        gain_grads[2],
        ffn_gate_grad,
        ffn_up_grad,
        ffn_down_grad,
    )


def solution(mesh):
    in_specs = (
        P("fsdp", "ctx", None),
        P("fsdp", "ctx", None),
        P("fsdp", None),
        P("fsdp", None),
        P(),
        P("fsdp", "ctx", None),
        P("fsdp"),
        P("fsdp", "tp"),
        P("fsdp", "tp"),
        P("fsdp", "tp"),
        P("tp", "fsdp"),
        P("fsdp", "tp"),
        P("fsdp"),
        P("fsdp", "tp"),
        P("fsdp", "tp"),
        P("fsdp", "tp"),
        P("tp", "fsdp"),
        P("fsdp"),
        P("fsdp", "tp"),
        P("fsdp", "tp"),
        P("tp", "fsdp"),
    )
    out_specs = (
        P("fsdp", "ctx", None),
        P("fsdp", "ctx", None),
        P("fsdp", "ctx", None),
        P("fsdp"),
        P("fsdp", "tp"),
        P("fsdp", "tp"),
        P("fsdp", "tp"),
        P("tp", "fsdp"),
        P("fsdp", "tp"),
        P("fsdp"),
        P("fsdp", "tp"),
        P("fsdp", "tp"),
        P("fsdp", "tp"),
        P("tp", "fsdp"),
        P("fsdp"),
        P("fsdp", "tp"),
        P("fsdp", "tp"),
        P("tp", "fsdp"),
    )
    return jax.shard_map(body, mesh=mesh, in_specs=in_specs, out_specs=out_specs, check_vma=False)
```
